256 devices in a mesh: row: 16 (over x, z_hi), col: 16 (over y, z_lo, core).
Axes of the slice: x: 4, y: 4, z: 8 (z_hi: 4, z_lo: 2; z = z_hi * 2 + z_lo), core: 2. Of those that a mesh axis runs over, the one named last changes fastest.
Arguments:
- positions: float32 [3, 65536], P(None, ('row', 'col')), may hold values from -6 to 6
- features: bfloat16 [128, 65536], P(None, ('row', 'col')), may hold values from -6 to 6
- fill: int32 [512], P(('row', 'col')), may hold values from 64 to 128, as said below
- tiles: int32 [2048, 2], P(('row', 'col')), may hold values from 0 to 31, as said below
- tile_count: int32 [256], P(('row', 'col')), may hold values from 2 to 8, as said below
- w_radial: float32 [64, 32], replicated, may hold values from -1 to 1
- w_left: bfloat16 [128, 64], replicated, may hold values from -0.5 to 0.5
- w_right: bfloat16 [128, 64], replicated, may hold values from -0.5 to 0.5
- w_hidden: bfloat16 [64, 64], replicated, may hold values from -0.75 to 0.75
- w_out: bfloat16 [64], replicated, may hold values from -0.25 to 0.25
Outputs:
- forces: float32 [3, 65536], P(None, ('row', 'col'))
- bead_energy: float32 [65536], P(('row', 'col'))
The draws below stay inside these ranges and needn't reach their ends.
Inputs may be any that keep to these rules, and one draw needn't show every extreme that they name: `fill`: at least 64; some cluster holds 128. `tiles`: A device's 8 slots name distinct cluster pairs; the first entry is below 32, the second below 32; some device has the pair of the last clusters of both groups. `tile_count`: at least 2; some device has all 8 slots live.
All inputs are finite; a program needn't handle non-finite values.
Results may differ from the reference program's by a relative error of at most 0.0045.
Values may be sent and summed in bfloat16 or wider, within the bound.
No kernel may reach another device: no remote copies, remote signals or barrier semaphores. Data moves between devices by JAX's collectives and lax.ppermute only.
A program may use at most 64 MiB of HBM per device.

```python
import jax
import jax.numpy as jnp
from jax import lax

CL = 128
HID = 64
EMB = 128
NRBF = 32
CPD = 2
MAXT = 8
NC = 512
NB = 65536
GR = 32
GC = 32
NTILES = 2048
N_COL = 16


def draw_fill(key, part):
    counts = jax.random.randint(jax.random.fold_in(key, 11), (NC,), CL // 2, CL + 1)
    where = jax.random.randint(jax.random.fold_in(key, 12), (), 0, NC)
    return counts.at[where].set(CL).astype(jnp.int32)


def draw_tiles(key, part):
    devices = NTILES // MAXT
    chosen = jax.random.randint(jax.random.fold_in(key, 22), (), 0, devices)
    corner = GR * GC - 1

    def one(index):
        order = jax.random.permutation(jax.random.fold_in(jax.random.fold_in(key, 21), index), GR * GC)[:MAXT]
        present = jnp.any(order == corner)
        forced = jnp.where(present, order, order.at[0].set(corner))
        order = jnp.where(index == chosen, forced, order)
        return jnp.stack([order // GC, order % GC], 1)
    return jax.vmap(one)(jnp.arange(devices)).reshape(NTILES, 2).astype(jnp.int32)


def draw_tile_count(key, part):
    devices = NTILES // MAXT
    counts = jax.random.randint(jax.random.fold_in(key, 31), (devices,), 2, MAXT + 1)
    where = jax.random.randint(jax.random.fold_in(key, 32), (), 0, devices)
    return counts.at[where].set(MAXT).astype(jnp.int32)


def steps_of(own_key, dims, shards, least, largest):
    level = 1.0
    for position, parts in shards:
        heights = jax.random.uniform(jax.random.fold_in(jax.random.fold_in(own_key, 6), position), (parts,), jnp.float32, least / len(shards), largest / len(shards))
        level = level * jnp.repeat(jnp.exp(heights), dims[position] // parts).reshape((-1,) + (1,) * (len(dims) - 1 - position))
    return level


def gaussian(rng, extent, deviation, limit, cuts=(), kind=jnp.bfloat16):
    level = steps_of(rng, extent, cuts, -0.22, 0.18) if cuts else 1.0
    drawn = jax.random.normal(rng, extent, jnp.float32) * deviation * level
    return jnp.minimum(jnp.maximum(drawn, -limit), limit).astype(kind)


def setup_inputs(seed: int = 0) -> dict:
    streams_of = jax.random.split(jax.random.key(seed), 11)
    positions = gaussian(streams_of[0], (3, NB), 1.0, 6.0, ((1, 256),), jnp.float32)
    features = gaussian(streams_of[1], (EMB, NB), 1.0, 6.0, ((1, 256),))
    fill = draw_fill(jax.random.fold_in(streams_of[10], 71), 0)
    tiles = draw_tiles(jax.random.fold_in(streams_of[10], 71), 0)
    tile_count = draw_tile_count(jax.random.fold_in(streams_of[10], 71), 0)
    w_radial = gaussian(streams_of[5], (HID, NRBF), NRBF ** -0.5, 1.0, (), jnp.float32)
    w_left = gaussian(streams_of[6], (EMB, HID), EMB ** -0.5, 0.5)
    w_right = gaussian(streams_of[7], (EMB, HID), EMB ** -0.5, 0.5)
    w_hidden = gaussian(streams_of[8], (HID, HID), HID ** -0.5, 0.75)
    w_out = gaussian(streams_of[9], (HID,), (HID * 8) ** -0.5, 0.25)
    return dict(positions=positions, features=features, fill=fill, tiles=tiles, tile_count=tile_count, w_radial=w_radial, w_left=w_left, w_right=w_right, w_hidden=w_hidden, w_out=w_out)


SOFT = 0.01
RANGE = 6.0

def dsilu(value):
    sig = jax.nn.sigmoid(value)
    return sig * (1.0 + value * (1.0 - sig))

def tile_terms(left, right, proj_a, proj_b, same, live_tile, w_radial, w_hidden, w_out):
    slots = left.shape[1]
    hidden = w_radial.shape[0]
    nbasis = w_radial.shape[1]
    delta = left[:3, :, None] - right[:3, None, :]
    dist = jnp.sqrt(lax.optimization_barrier(jnp.sum(delta * delta, 0)) + SOFT)
    ident = (jnp.arange(slots)[:, None] == jnp.arange(slots)[None, :]).astype(jnp.float32)
    mask = left[3][:, None] * right[3][None, :] * (1.0 - same * ident) * live_tile
    flat = dist.reshape(-1)
    centers = RANGE * jnp.arange(nbasis, dtype=jnp.float32) / (nbasis - 1)
    sharp = ((nbasis - 1) / RANGE) ** 2
    offset = flat[None, :] - centers[:, None]
    basis = jnp.exp(-sharp * offset * offset)
    pair_in = (proj_a.astype(jnp.float32)[:, :, None] + proj_b.astype(jnp.float32)[:, None, :]).reshape(hidden, -1)
    pre1 = jnp.dot(w_radial, basis, precision=lax.Precision.HIGHEST) + pair_in
    act1 = jax.nn.silu(pre1).astype(jnp.bfloat16)
    pre2 = jnp.dot(w_hidden, act1, preferred_element_type=jnp.float32)
    act2 = jax.nn.silu(pre2).astype(jnp.bfloat16)
    energy = jnp.dot(w_out[None, :], act2, preferred_element_type=jnp.float32)[0]
    back2 = (w_out.astype(jnp.float32)[:, None] * dsilu(pre2)).astype(jnp.bfloat16)
    back1 = lax.dot_general(w_hidden, back2, (((0,), (0,)), ((), ())), preferred_element_type=jnp.float32) * dsilu(pre1)
    radial = lax.dot_general(w_radial, back1, (((0,), (0,)), ((), ())), precision=lax.Precision.HIGHEST)
    slope = lax.optimization_barrier(jnp.sum(radial * basis * (-2.0 * sharp * offset), 0))
    weight = mask * slope.reshape(slots, slots) / dist
    energy_left = lax.optimization_barrier(jnp.sum(mask * energy.reshape(slots, slots), 1))
    pos_left = left[:3]
    pos_right = right[:3]
    force_left = jnp.dot(pos_right, weight.T, precision=lax.Precision.HIGHEST) - pos_left * lax.optimization_barrier(jnp.sum(weight, 1))[None, :]
    force_right = jnp.dot(pos_left, weight, precision=lax.Precision.HIGHEST) - pos_right * lax.optimization_barrier(jnp.sum(weight, 0))[None, :]
    return (force_left, energy_left, force_right)

def reference(positions, features, fill, tiles, tile_count, w_radial, w_left, w_right, w_hidden, w_out):
    live = (jnp.arange(CL, dtype=jnp.int32)[None, :] < fill[:, None]).astype(jnp.float32).reshape(NB)
    coords = jnp.concatenate([positions, live[None, :]], 0)
    proj_left = lax.dot_general(w_left, features, (((0,), (0,)), ((), ())), preferred_element_type=jnp.float32).astype(jnp.bfloat16)
    proj_right = lax.dot_general(w_right, features, (((0,), (0,)), ((), ())), preferred_element_type=jnp.float32).astype(jnp.bfloat16)

    def step(carry, slot):
        firsts, seconds = carry
        device = slot // MAXT
        row_index = device // N_COL
        col_index = device % N_COL
        first = (row_index * GR + tiles[slot, 0]).astype(jnp.int32)
        other = tiles[slot, 1]
        second = ((other // CPD * N_COL + col_index) * CPD + other % CPD).astype(jnp.int32)
        is_live = slot % MAXT < tile_count[device]

        def work(carry):
            firsts, seconds = carry
            start_a = (first * CL).astype(jnp.int32)
            start_b = (second * CL).astype(jnp.int32)
            left = lax.dynamic_slice_in_dim(coords, start_a, CL, 1)
            right = lax.dynamic_slice_in_dim(coords, start_b, CL, 1)
            part_a = lax.dynamic_slice_in_dim(proj_left, start_a, CL, 1)
            part_b = lax.dynamic_slice_in_dim(proj_right, start_b, CL, 1)
            same = (first == second).astype(jnp.float32)
            force_a, energy_a, force_b = tile_terms(left, right, part_a, part_b, same, jnp.float32(1.0), w_radial, w_hidden, w_out)
            added = jnp.concatenate([force_a, energy_a[None, :]], 0)
            firsts = lax.dynamic_update_slice_in_dim(firsts, lax.dynamic_slice_in_dim(firsts, start_a, CL, 1) + added, start_a, 1)
            seconds = lax.dynamic_update_slice_in_dim(seconds, lax.dynamic_slice_in_dim(seconds, start_b, CL, 1) + force_b, start_b, 1)
            return (firsts, seconds)
        return (lax.cond(is_live, work, lambda carry: carry, (firsts, seconds)), None)
    start = (jnp.zeros((4, NB), jnp.float32), jnp.zeros((3, NB), jnp.float32))
    (firsts, seconds), unused = lax.scan(step, start, jnp.arange(NTILES, dtype=jnp.int32))
    return (firsts[:3] + seconds, firsts[3])
```

```python
import functools

import jax
import jax.numpy as jnp
from jax import lax
from jax.experimental import pallas as pl
from jax.experimental.pallas import tpu as pltpu
from jax.sharding import PartitionSpec as P

CL = 128
CPD = 2
HID = 64
NRBF = 32
PAY = 80
ROWS = 16
SOFT = 0.01
RANGE = 6.0
SHARP = ((NRBF - 1) / RANGE) ** 2
LOG2E = 1.4426950408889634
SCALE = (SHARP * LOG2E) ** 0.5

F32 = jnp.float32
BF16 = jnp.bfloat16


def pack_kernel(fill_ref, pos_ref, feat_ref, wl_ref, wr_ref, left_ref, right_ref):
    peers = left_ref.shape[0]
    feat = feat_ref[...]
    pos = pos_ref[...]
    high = pos.astype(BF16).astype(F32)
    rest = pos - high
    mid = rest.astype(BF16).astype(F32)
    low = (rest - mid).astype(BF16).astype(F32)
    lane = lax.broadcasted_iota(jnp.int32, (1, CL), 1)
    for weight_ref, out_ref in ((wl_ref, left_ref), (wr_ref, right_ref)):
        proj = jnp.dot(weight_ref[...], feat, preferred_element_type=F32)
        for k in range(CPD):
            cut = slice(k * CL, (k + 1) * CL)
            live = (lane < fill_ref[k]).astype(F32)
            extra = jnp.concatenate(
                [high[:, cut], mid[:, cut], low[:, cut], live, jnp.zeros((6, CL), F32)], 0
            )
            both = jnp.concatenate([proj[:, cut], extra], 0).astype(BF16)
            for peer in range(peers):
                out_ref[peer, k] = both


def split(value):
    high = value.astype(BF16)
    return high, (value - high.astype(F32)).astype(BF16)


def unpack(block):
    block = block.astype(F32)
    extra = block[HID:]
    pos = extra[0:3] + extra[3:6] + extra[6:9]
    return block[:HID], pos, extra[9:10]


def tile_kernel(
    tiles_ref, count_ref, base_ref, left_ref, right_ref, wr_ref, wh_ref, wht_ref, wo_ref,
    first_ref, second_ref, mix_ref, head_ref, turned_ref, sides_ref,
):
    first_ref[...] = jnp.zeros_like(first_ref)
    second_ref[...] = jnp.zeros_like(second_ref)
    w_radial = wr_ref[...].T
    w_high, w_low = split(0.5 * w_radial)
    t_high, t_low = split(w_radial * (-SHARP / SCALE))
    mix = jnp.concatenate([w_high, w_high, w_low], 1)
    mix_ref[...] = jnp.concatenate([t_high, t_high, t_low], 1)
    wh = wh_ref[...]
    wht = wht_ref[...]
    wo = wo_ref[...]
    wo_half = jnp.broadcast_to(0.5 * wo, (HID, 2 * CL))
    wo_full = jnp.broadcast_to(wo, (HID, 2 * CL))
    centers = (
        lax.broadcasted_iota(jnp.int32, (NRBF, 2 * CL), 0).astype(F32) * (RANGE / (NRBF - 1) * SCALE)
    )
    sub = lax.broadcasted_iota(jnp.int32, (ROWS, CL), 0)
    lane = lax.broadcasted_iota(jnp.int32, (ROWS, CL), 1)

    def tile(slot, carry):
        first = tiles_ref[0, slot]
        other = tiles_ref[1, slot]
        same = base_ref[0] + first == (other // CPD * base_ref[2] + base_ref[1]) * CPD + other % CPD
        same = same.astype(F32)
        proj_a, pos_a, live_a = unpack(left_ref[first])
        proj_b, pos_b, live_b = unpack(right_ref[other])
        fill_a = jnp.sum(live_a).astype(jnp.int32)
        half_a = (0.5 * proj_a).astype(BF16)
        for g in range(CL // ROWS):
            head_ref[g] = jnp.concatenate([mix, half_a[:, g * ROWS : (g + 1) * ROWS]], 1)
        turned_ref[...] = jnp.concatenate([pos_a, live_a, jnp.zeros((CL - 4, CL), F32)], 0).T
        sides_ref[...] = jnp.zeros_like(sides_ref)
        add_b = jnp.concatenate([0.5 * proj_b] * 2, 1)

        def block(g, sums):
            start = pl.multiple_of(g * ROWS, ROWS)
            mine = turned_ref[pl.ds(start, ROWS), :]
            delta = [mine[:, c : c + 1] - pos_b[c : c + 1] for c in range(3)]
            dist = jnp.sqrt(delta[0] * delta[0] + delta[1] * delta[1] + delta[2] * delta[2] + SOFT)
            scaled = dist * SCALE
            head = head_ref[g]
            tail = mix_ref[...]
            slopes = []
            energies = []
            for c in range(ROWS // 2):
                row = jnp.concatenate([scaled[2 * c : 2 * c + 1], scaled[2 * c + 1 : 2 * c + 2]], 1)
                offset = row - centers
                basis = jnp.exp2(-(offset * offset))
                b_high, b_low = split(basis)
                d_high, d_low = split(basis * offset)
                sel = lax.broadcasted_iota(jnp.int32, (ROWS, 2 * CL), 0)
                which = lax.broadcasted_iota(jnp.int32, (ROWS, 2 * CL), 1) // CL + 2 * c
                pick = (sel == which).astype(F32).astype(BF16)
                stacked = jnp.concatenate([b_high, b_low, b_high, pick], 0)
                half1 = jnp.dot(head, stacked, preferred_element_type=F32) + add_b
                tangent = jnp.dot(
                    tail, jnp.concatenate([d_high, d_low, d_high], 0), preferred_element_type=F32
                )
                up1 = 1.0 + jnp.tanh(half1)
                silu1 = half1 * up1
                grad1 = up1 + silu1 * (2.0 - up1)
                half2 = jnp.dot(wh, silu1.astype(BF16), preferred_element_type=F32)
                up2 = 1.0 + jnp.tanh(half2)
                silu2 = half2 * up2
                grad2 = up2 + silu2 * (2.0 - up2)
                back2 = (wo_half * grad2).astype(BF16)
                back1 = jnp.dot(wht, back2, preferred_element_type=F32)
                slope = jnp.sum(back1 * (grad1 * tangent), 0, keepdims=True)
                energy = jnp.sum(silu2.astype(BF16).astype(F32) * wo_full, 0, keepdims=True)
                slopes += [slope[:, :CL], slope[:, CL:]]
                energies += [energy[:, :CL], energy[:, CL:]]
            slope = jnp.concatenate(slopes, 0)
            energy = jnp.concatenate(energies, 0)
            mask = mine[:, 3:4] * live_b * (1.0 - same * (sub + start == lane).astype(F32))
            weight = mask * slope / dist
            pulls = [weight * d for d in delta]
            parts = [jnp.sum(p, 1, keepdims=True) for p in pulls]
            parts.append(jnp.sum(mask * energy, 1, keepdims=True))
            side = jnp.zeros((ROWS, CL), F32)
            for c in range(4):
                sign = -1.0 if c < 3 else 1.0
                side = jnp.where(lane == c, sign * parts[c], side)
            sides_ref[pl.ds(start, ROWS), :] = side
            return tuple(s + p for s, p in zip(sums, pulls))

        blank = jnp.zeros((ROWS, CL), F32)
        sums = lax.fori_loop(0, (fill_a + ROWS - 1) // ROWS, block, (blank, blank, blank))
        firsts = sides_ref[...].T[:4]
        seconds = jnp.concatenate(
            [jnp.sum(s, 0, keepdims=True) for s in sums] + [jnp.zeros((1, CL), F32)], 0
        )
        row8 = lax.broadcasted_iota(jnp.int32, (8, CL), 0) // 4
        first_ref[first // CPD] += jnp.where(row8 == first % CPD, jnp.concatenate([firsts] * 2, 0), 0.0)
        second_ref[other // CPD] += jnp.where(
            row8 == other % CPD, jnp.concatenate([seconds] * 2, 0), 0.0
        )
        return carry

    lax.fori_loop(0, count_ref[0], tile, 0)


def add_kernel(first_ref, second_ref, force_ref, energy_ref):
    total = first_ref[0]
    other = second_ref[0]
    for peer in range(1, first_ref.shape[0]):
        total = total + first_ref[peer]
    for peer in range(1, second_ref.shape[0]):
        other = other + second_ref[peer]
    force = total + other
    for k in range(CPD):
        cut = slice(k * CL, (k + 1) * CL)
        force_ref[:, cut] = force[4 * k : 4 * k + 3]
        energy_ref[:, cut] = total[4 * k + 3 : 4 * k + 4]


def body(positions, features, fill, tiles, tile_count, w_radial, w_left, w_right, w_hidden, w_out):
    rows = lax.axis_size("row")
    cols = lax.axis_size("col")
    smem = pl.BlockSpec(memory_space=pltpu.SMEM)
    vmem = pl.BlockSpec(memory_space=pltpu.VMEM)
    with jax.named_scope("pack"):
        left, right = pl.pallas_call(
            pack_kernel,
            out_shape=(
                jax.ShapeDtypeStruct((cols, CPD, PAY, CL), BF16),
                jax.ShapeDtypeStruct((rows, CPD, PAY, CL), BF16),
            ),
            in_specs=[smem] + [vmem] * 4,
            out_specs=(vmem, vmem),
        )(fill, positions, features, w_left.T, w_right.T)
    with jax.named_scope("spread"):
        left = lax.all_to_all(left, "col", 0, 0).reshape(cols * CPD, PAY, CL)
        right = lax.all_to_all(right, "row", 0, 0).reshape(rows * CPD, PAY, CL)
    base = jnp.stack([lax.axis_index("row") * cols * CPD, lax.axis_index("col"), jnp.int32(cols)])
    with jax.named_scope("tiles"):
        firsts, seconds = pl.pallas_call(
            tile_kernel,
            out_shape=(
                jax.ShapeDtypeStruct((cols, 8, CL), F32),
                jax.ShapeDtypeStruct((rows, 8, CL), F32),
            ),
            in_specs=[smem] * 3 + [vmem] * 6,
            out_specs=(vmem, vmem),
            scratch_shapes=[
                pltpu.VMEM((HID, 3 * NRBF), BF16),
                pltpu.VMEM((CL // ROWS, HID, 3 * NRBF + ROWS), BF16),
                pltpu.VMEM((CL, CL), F32),
                pltpu.VMEM((CL, CL), F32),
            ],
            compiler_params=pltpu.CompilerParams(vmem_limit_bytes=48 * 1024 * 1024),
        )(
            tiles.T, tile_count, base, left, right, w_radial.T,
            w_hidden * 0.5, w_hidden.T, w_out.astype(F32)[:, None],
        )
    with jax.named_scope("collect"):
        firsts = lax.all_to_all(firsts, "col", 0, 0)
        seconds = lax.all_to_all(seconds, "row", 0, 0)
    with jax.named_scope("add"):
        force, energy = pl.pallas_call(
            add_kernel,
            out_shape=(
                jax.ShapeDtypeStruct((3, CPD * CL), F32),
                jax.ShapeDtypeStruct((1, CPD * CL), F32),
            ),
        )(firsts, seconds)
    return force, energy.reshape(CPD * CL)


def solution(mesh):
    return jax.shard_map(
        body,
        mesh=mesh,
        in_specs=(
            P(None, ("row", "col")),
            P(None, ("row", "col")),
            P(("row", "col")),
            P(("row", "col"), None),
            P(("row", "col")),
            P(),
            P(),
            P(),
            P(),
            P(),
        ),
        out_specs=(P(None, ("row", "col")), P(("row", "col"))),
        check_vma=False,
    )
```

```python
import functools

import jax
import jax.numpy as jnp
from jax import lax
from jax.experimental import pallas as pl
from jax.experimental.pallas import tpu as pltpu
from jax.sharding import PartitionSpec as P

CL = 128
CPD = 2
HID = 64
NRBF = 32
PAY = 80
ROWS = 16
SOFT = 0.01
RANGE = 6.0
SHARP = ((NRBF - 1) / RANGE) ** 2
LOG2E = 1.4426950408889634
SCALE = (SHARP * LOG2E) ** 0.5

F32 = jnp.float32
BF16 = jnp.bfloat16


def pack_kernel(fill_ref, pos_ref, feat_ref, wl_ref, wr_ref, left_ref, right_ref):
    peers = left_ref.shape[0]
    feat = feat_ref[...]
    pos = pos_ref[...]
    high = pos.astype(BF16).astype(F32)
    rest = pos - high
    mid = rest.astype(BF16).astype(F32)
    low = (rest - mid).astype(BF16).astype(F32)
    lane = lax.broadcasted_iota(jnp.int32, (1, CL), 1)
    for weight_ref, out_ref in ((wl_ref, left_ref), (wr_ref, right_ref)):
        proj = jnp.dot(weight_ref[...], feat, preferred_element_type=F32)
        for k in range(CPD):
            cut = slice(k * CL, (k + 1) * CL)
            live = (lane < fill_ref[k]).astype(F32)
            extra = jnp.concatenate(
                [high[:, cut], mid[:, cut], low[:, cut], live, jnp.zeros((6, CL), F32)], 0
            )
            both = jnp.concatenate([proj[:, cut], extra], 0).astype(BF16)
            for peer in range(peers):
                out_ref[peer, k] = both


def unpack(block):
    block = block.astype(F32)
    extra = block[HID:]
    pos = extra[0:3] + extra[3:6] + extra[6:9]
    return block[:HID], pos, extra[9:10]


def spread4(value):
    rows, cols = value.shape
    tall = jnp.concatenate([value] * 4, 0)
    wide = jnp.concatenate([tall] * 4, 1)
    down = lax.broadcasted_iota(jnp.int32, wide.shape, 0) // rows
    across = lax.broadcasted_iota(jnp.int32, wide.shape, 1) // cols
    return jnp.where(down == across, wide, 0.0)


def tile_kernel(
    tiles_ref, count_ref, base_ref, left_ref, right_ref, wr_ref, wh_ref, wo_ref,
    first_ref, second_ref,
    radial_ref, tangent_ref, hidden_ref, back_ref, out_ref, pick_ref, head_ref, adds_ref,
    turned_ref, across_ref, slopes_ref, energies_ref, half1_ref, rate_ref, half2_ref, chain_ref, blocks_ref,
):
    count = count_ref[0]
    wide = 2 * CL
    first_ref[...] = jnp.zeros_like(first_ref)
    second_ref[...] = jnp.zeros_like(second_ref)
    w_radial = wr_ref[...].T
    for into_ref, scale in ((radial_ref, 0.5), (tangent_ref, -SHARP / SCALE)):
        full = spread4(scale * w_radial)
        high = full.astype(BF16).astype(F32)
        into_ref[...] = jnp.concatenate([high, full - high], 1).astype(BF16)
    w_hidden = wh_ref[...].astype(F32)
    w_out = wo_ref[...]
    hidden_ref[...] = spread4(0.5 * w_hidden).astype(BF16)
    back_ref[...] = spread4(w_hidden.T).astype(BF16)
    half_out = jnp.broadcast_to(jnp.concatenate([0.5 * w_out] * 4, 0), (4 * HID, wide))
    flat_out = jnp.concatenate([w_out.T] * 4, 1)
    lane8 = lax.broadcasted_iota(jnp.int32, (8, 4 * HID), 1) // HID
    sub8 = lax.broadcasted_iota(jnp.int32, (8, 4 * HID), 0)
    out_ref[...] = jnp.where(lane8 == sub8, flat_out, 0.0).astype(BF16)
    quad = lax.broadcasted_iota(jnp.int32, (CL, wide), 0) // 4
    side = lax.broadcasted_iota(jnp.int32, (CL, wide), 1) // CL
    for g in range(CL // 8):
        pick_ref[g] = (quad == 2 * g + side).astype(F32).astype(BF16)
    centers = (
        lax.broadcasted_iota(jnp.int32, (NRBF, wide), 0).astype(F32) * (RANGE / (NRBF - 1) * SCALE)
    )
    ident = (
        lax.broadcasted_iota(jnp.int32, (HID, HID), 0)
        == lax.broadcasted_iota(jnp.int32, (HID, HID), 1)
    ).astype(F32)
    lane4 = lax.broadcasted_iota(jnp.int32, (HID, CL), 1) % 4

    def prepare(slot, carry):
        proj_a, pos_a, live_a = unpack(left_ref[tiles_ref[0, slot]])
        proj_b, pos_b, live_b = unpack(right_ref[tiles_ref[1, slot]])
        half_a = 0.5 * proj_a
        cols = jnp.concatenate([jnp.where(lane4 == q, half_a, 0.0) for q in range(4)], 0)
        head_ref[slot] = jnp.concatenate([cols, jnp.concatenate([ident] * 4, 0)], 1).astype(BF16)
        adds_ref[slot] = jnp.concatenate([0.5 * proj_b] * 2, 1).astype(BF16)
        turned_ref[slot] = jnp.concatenate([pos_a, live_a, jnp.zeros((CL - 4, CL), F32)], 0).T
        across_ref[slot] = jnp.concatenate([pos_b, live_b, jnp.zeros((4, CL), F32)], 0)
        fill_a = jnp.sum(live_a).astype(jnp.int32)
        blocks_ref[slot] = (fill_a + ROWS - 1) // ROWS
        return carry

    lax.fori_loop(0, count, prepare, 0)

    def distances(mine, across):
        delta = [mine[:, c : c + 1] - across[c : c + 1] for c in range(3)]
        dist = jnp.sqrt(delta[0] * delta[0] + delta[1] * delta[1] + delta[2] * delta[2] + SOFT)
        return delta, dist

    def enter(slot, g):
        start = pl.multiple_of(g * ROWS, ROWS)
        mine = turned_ref[slot, pl.ds(start, ROWS), :]
        scaled = distances(mine, across_ref[slot])[1] * SCALE
        head = jnp.concatenate([radial_ref[...], head_ref[slot]], 1)
        for e in range(ROWS // 8):
            bases = []
            rates = []
            for q in range(4):
                r = 8 * e + q
                row = jnp.concatenate([scaled[r : r + 1], scaled[r + 4 : r + 5]], 1)
                offset = row - centers
                basis = jnp.exp2(-(offset * offset))
                bases.append(basis.astype(BF16))
                rates.append((basis * offset).astype(BF16))
            tail = jnp.concatenate(
                bases + bases + [pick_ref[g * (ROWS // 8) + e], adds_ref[slot]], 0
            )
            half1_ref[e] = jnp.dot(head, tail, preferred_element_type=F32)
            rate_ref[e] = jnp.dot(
                tangent_ref[...], jnp.concatenate(rates + rates, 0), preferred_element_type=F32
            )

    def middle():
        for e in range(ROWS // 8):
            half1 = half1_ref[e]
            up1 = 1.0 + jnp.tanh(half1)
            silu1 = half1 * up1
            grad1 = up1 + silu1 * (2.0 - up1)
            chain_ref[e] = grad1 * rate_ref[e]
            half2_ref[e] = jnp.dot(hidden_ref[...], silu1.astype(BF16), preferred_element_type=F32)

    def leave(slot, g):
        for e in range(ROWS // 8):
            half2 = half2_ref[e]
            up2 = 1.0 + jnp.tanh(half2)
            silu2 = half2 * up2
            grad2 = up2 + silu2 * (2.0 - up2)
            back1 = jnp.dot(back_ref[...], (half_out * grad2).astype(BF16), preferred_element_type=F32)
            energy = jnp.dot(out_ref[...], silu2.astype(BF16), preferred_element_type=F32)
            terms = back1 * chain_ref[e]
            lines = jnp.concatenate(
                [jnp.sum(terms[q * HID : (q + 1) * HID], 0, keepdims=True) for q in range(4)], 0
            )
            at = pl.ds(pl.multiple_of(g * ROWS + 8 * e, 8), 8)
            slopes_ref[slot, at, :] = jnp.concatenate([lines[:, :CL], lines[:, CL:]], 0)
            energies_ref[slot, at, :] = jnp.concatenate([energy[:4, :CL], energy[:4, CL:]], 0)

    spare = slopes_ref.shape[0] - 1

    def step(carry):
        slot, g, slot1, g1, slot2, g2, left = carry
        leave(slot2, g2)
        middle()
        enter(slot, g)
        last = g + 1 >= blocks_ref[slot]
        ended = jnp.logical_and(last, slot + 1 >= count)
        slot2, g2 = slot1, g1
        slot1 = jnp.where(left > 2, slot, spare)
        g1 = g
        g = jnp.where(ended, g, jnp.where(last, 0, g + 1))
        slot = jnp.where(jnp.logical_and(last, jnp.logical_not(ended)), slot + 1, slot)
        return slot, g, slot1, g1, slot2, g2, left - 1

    total = lax.fori_loop(0, count, lambda slot, n: n + blocks_ref[slot], 0)
    zero = jnp.int32(0)
    far = jnp.int32(spare)
    lax.while_loop(
        lambda carry: carry[6] > 0, step, (zero, zero, far, zero, far, zero, total + 2)
    )

    sub = lax.broadcasted_iota(jnp.int32, (CL, CL), 0)
    lane = lax.broadcasted_iota(jnp.int32, (CL, CL), 1)
    row8 = lax.broadcasted_iota(jnp.int32, (8, CL), 0) // 4

    def finish(slot, carry):
        first = tiles_ref[0, slot]
        other = tiles_ref[1, slot]
        same = base_ref[0] + first == (other // CPD * base_ref[2] + base_ref[1]) * CPD + other % CPD
        mine = turned_ref[slot]
        across = across_ref[slot]
        delta, dist = distances(mine, across)
        mask = mine[:, 3:4] * across[3:4]
        keep = jnp.logical_and(mask > 0.0, jnp.logical_or(jnp.logical_not(same), sub != lane))
        weight = jnp.where(keep, slopes_ref[slot] / dist, 0.0)
        pulls = [weight * d for d in delta]
        parts = [-jnp.sum(p, 1, keepdims=True) for p in pulls]
        parts.append(jnp.sum(jnp.where(keep, energies_ref[slot], 0.0), 1, keepdims=True))
        side = jnp.zeros((CL, CL), F32)
        for c in range(4):
            side = jnp.where(lane == c, parts[c], side)
        firsts = side.T[:4]
        seconds = jnp.concatenate(
            [jnp.sum(p, 0, keepdims=True) for p in pulls] + [jnp.zeros((1, CL), F32)], 0
        )
        first_ref[first // CPD] += jnp.where(row8 == first % CPD, jnp.concatenate([firsts] * 2, 0), 0.0)
        second_ref[other // CPD] += jnp.where(
            row8 == other % CPD, jnp.concatenate([seconds] * 2, 0), 0.0
        )
        return carry

    lax.fori_loop(0, count, finish, 0)


def tile_call(tiles, tile_count, base, left, right, w_radial, w_hidden, w_out):
    smem = pl.BlockSpec(memory_space=pltpu.SMEM)
    vmem = pl.BlockSpec(memory_space=pltpu.VMEM)
    slots = tiles.shape[0]
    groups = ROWS // 8
    hid4 = 4 * HID
    wide = 2 * CL
    return pl.pallas_call(
        tile_kernel,
        name="tiles",
        out_shape=(
            jax.ShapeDtypeStruct((left.shape[0] // CPD, 8, CL), F32),
            jax.ShapeDtypeStruct((right.shape[0] // CPD, 8, CL), F32),
        ),
        in_specs=[smem] * 3 + [vmem] * 5,
        out_specs=(vmem, vmem),
        scratch_shapes=[
            pltpu.VMEM((hid4, 8 * NRBF), BF16),
            pltpu.VMEM((hid4, 8 * NRBF), BF16),
            pltpu.VMEM((hid4, hid4), BF16),
            pltpu.VMEM((hid4, hid4), BF16),
            pltpu.VMEM((8, hid4), BF16),
            pltpu.VMEM((CL // 8, CL, wide), BF16),
            pltpu.VMEM((slots, hid4, CL + HID), BF16),
            pltpu.VMEM((slots, HID, wide), BF16),
            pltpu.VMEM((slots, CL, CL), F32),
            pltpu.VMEM((slots, 8, CL), F32),
            pltpu.VMEM((slots + 1, CL, CL), F32),
            pltpu.VMEM((slots + 1, CL, CL), F32),
            pltpu.VMEM((groups, hid4, wide), F32),
            pltpu.VMEM((groups, hid4, wide), F32),
            pltpu.VMEM((groups, hid4, wide), F32),
            pltpu.VMEM((groups, hid4, wide), F32),
            pltpu.SMEM((slots,), jnp.int32),
        ],
        compiler_params=pltpu.CompilerParams(vmem_limit_bytes=48 * 1024 * 1024),
    )(
        tiles.T, tile_count, base, left, right, w_radial.T, w_hidden, w_out.astype(F32)[:, None],
    )


def add_kernel(first_ref, second_ref, force_ref, energy_ref):
    total = first_ref[0]
    other = second_ref[0]
    for peer in range(1, first_ref.shape[0]):
        total = total + first_ref[peer]
    for peer in range(1, second_ref.shape[0]):
        other = other + second_ref[peer]
    force = total + other
    for k in range(CPD):
        cut = slice(k * CL, (k + 1) * CL)
        force_ref[:, cut] = force[4 * k : 4 * k + 3]
        energy_ref[:, cut] = total[4 * k + 3 : 4 * k + 4]


def body(positions, features, fill, tiles, tile_count, w_radial, w_left, w_right, w_hidden, w_out):
    rows = lax.axis_size("row")
    cols = lax.axis_size("col")
    smem = pl.BlockSpec(memory_space=pltpu.SMEM)
    vmem = pl.BlockSpec(memory_space=pltpu.VMEM)
    with jax.named_scope("pack"):
        left, right = pl.pallas_call(
            pack_kernel,
            out_shape=(
                jax.ShapeDtypeStruct((cols, CPD, PAY, CL), BF16),
                jax.ShapeDtypeStruct((rows, CPD, PAY, CL), BF16),
            ),
            in_specs=[smem] + [vmem] * 4,
            out_specs=(vmem, vmem),
        )(fill, positions, features, w_left.T, w_right.T)
    with jax.named_scope("spread"):
        left = lax.all_to_all(left, "col", 0, 0).reshape(cols * CPD, PAY, CL)
        right = lax.all_to_all(right, "row", 0, 0).reshape(rows * CPD, PAY, CL)
    base = jnp.stack([lax.axis_index("row") * cols * CPD, lax.axis_index("col"), jnp.int32(cols)])
    with jax.named_scope("tiles"):
        firsts, seconds = tile_call(
            tiles, tile_count, base, left, right, w_radial, w_hidden, w_out
        )
    with jax.named_scope("collect"):
        firsts = lax.all_to_all(firsts, "col", 0, 0)
        seconds = lax.all_to_all(seconds, "row", 0, 0)
    with jax.named_scope("add"):
        force, energy = pl.pallas_call(
            add_kernel,
            out_shape=(
                jax.ShapeDtypeStruct((3, CPD * CL), F32),
                jax.ShapeDtypeStruct((1, CPD * CL), F32),
            ),
        )(firsts, seconds)
    return force, energy.reshape(CPD * CL)


def solution(mesh):
    return jax.shard_map(
        body,
        mesh=mesh,
        in_specs=(
            P(None, ("row", "col")),
            P(None, ("row", "col")),
            P(("row", "col")),
            P(("row", "col"), None),
            P(("row", "col")),
            P(),
            P(),
            P(),
            P(),
            P(),
        ),
        out_specs=(P(None, ("row", "col")), P(("row", "col"))),
        check_vma=False,
    )
```

```python
import functools

import jax
import jax.numpy as jnp
from jax import lax
from jax.experimental import pallas as pl
from jax.experimental.pallas import tpu as pltpu
from jax.sharding import PartitionSpec as P

CL = 128
CPD = 2
HID = 64
NRBF = 32
PAY = 80
LIVE = HID + 9
ROWS = 16
SOFT = 0.01
RANGE = 6.0
SHARP = ((NRBF - 1) / RANGE) ** 2
LOG2E = 1.4426950408889634
SCALE = (SHARP * LOG2E) ** 0.5

F32 = jnp.float32
BF16 = jnp.bfloat16


def pack_kernel(fill_ref, pos_ref, feat_ref, wl_ref, wr_ref, left_ref, right_ref):
    feat = feat_ref[...]
    pos = pos_ref[...]
    high = pos.astype(BF16).astype(F32)
    rest = pos - high
    mid = rest.astype(BF16).astype(F32)
    low = (rest - mid).astype(BF16).astype(F32)
    lane = lax.broadcasted_iota(jnp.int32, (1, CL), 1)
    for weight_ref, out_ref in ((wl_ref, left_ref), (wr_ref, right_ref)):
        proj = jnp.dot(weight_ref[...], feat, preferred_element_type=F32)
        for k in range(CPD):
            cut = slice(k * CL, (k + 1) * CL)
            live = (lane < fill_ref[k]).astype(F32)
            extra = jnp.concatenate(
                [high[:, cut], mid[:, cut], low[:, cut], live, jnp.zeros((6, CL), F32)], 0
            )
            both = jnp.concatenate([proj[:, cut], extra], 0).astype(BF16)
            for peer in range(out_ref.shape[0]):
                out_ref[peer, k] = both


def unpack(block):
    extra = block[HID:]
    pos = extra[0:3] + extra[3:6] + extra[6:9]
    return block[:HID], pos, extra[9:10]


def spread4(value):
    rows, cols = value.shape
    tall = jnp.concatenate([value] * 4, 0)
    wide = jnp.concatenate([tall] * 4, 1)
    down = lax.broadcasted_iota(jnp.int32, wide.shape, 0) // rows
    across = lax.broadcasted_iota(jnp.int32, wide.shape, 1) // cols
    return jnp.where(down == across, wide, 0.0)


def tile_kernel(
    tiles_ref, count_ref, base_ref, left_ref, right_ref, wr_ref, wh_ref, wo_ref,
    first_ref, second_ref,
    tangent_ref, hidden_ref, back_ref, out_ref, pick_ref, head_ref, adds_ref,
    turned_ref, across_ref, slopes_ref, energies_ref, half1_ref, rate_ref, half2_ref, chain_ref, blocks_ref, swaps_ref,
):
    count = count_ref[0]
    wide = 2 * CL
    first_ref[...] = jnp.zeros_like(first_ref)
    second_ref[...] = jnp.zeros_like(second_ref)
    w_radial = wr_ref[...].T
    radial = spread4(0.5 * w_radial)
    tangent_ref[...] = spread4(w_radial * (-SHARP / SCALE)).astype(BF16)
    w_hidden = wh_ref[...].astype(F32)
    w_out = wo_ref[...]
    hidden_ref[...] = spread4(0.5 * w_hidden).astype(BF16)
    back_ref[...] = spread4(w_hidden.T).astype(BF16)
    half_out = jnp.broadcast_to(jnp.concatenate([0.5 * w_out] * 4, 0), (4 * HID, wide))
    flat_out = jnp.concatenate([w_out.T] * 4, 1)
    lane8 = lax.broadcasted_iota(jnp.int32, (8, 4 * HID), 1) // HID
    sub8 = lax.broadcasted_iota(jnp.int32, (8, 4 * HID), 0)
    out_ref[...] = jnp.where(lane8 == sub8, flat_out, 0.0).astype(BF16)
    quad = lax.broadcasted_iota(jnp.int32, (HID, wide), 0) // 4
    side = lax.broadcasted_iota(jnp.int32, (HID, wide), 1) // CL
    for g in range(HID // 8):
        pick_ref[g] = (quad == 2 * g + side).astype(F32).astype(BF16)
    centers = (
        lax.broadcasted_iota(jnp.int32, (NRBF, wide), 0).astype(F32) * (RANGE / (NRBF - 1) * SCALE)
    )
    ident = (
        lax.broadcasted_iota(jnp.int32, (HID, HID), 0)
        == lax.broadcasted_iota(jnp.int32, (HID, HID), 1)
    ).astype(F32)
    lane4 = lax.broadcasted_iota(jnp.int32, (HID, CL), 1) % 4

    def prepare(slot, carry):
        first = tiles_ref[0, slot]
        away = jnp.bitwise_xor(first // CPD, base_ref[1])
        left = left_ref[away * CPD + first % CPD].astype(F32)
        other = tiles_ref[1, slot]
        beyond = jnp.bitwise_xor(other // CPD, base_ref[3])
        right = right_ref[beyond * CPD + other % CPD].astype(F32)
        fill_left = jnp.sum(left[LIVE : LIVE + 1]).astype(jnp.int32)
        fill_right = jnp.sum(right[LIVE : LIVE + 1]).astype(jnp.int32)
        swap = fill_right < fill_left
        swaps_ref[slot] = swap.astype(jnp.int32)
        proj_a, pos_a, live_a = unpack(jnp.where(swap, right, left))
        proj_b, pos_b, live_b = unpack(jnp.where(swap, left, right))
        half_a = 0.5 * proj_a
        cols = jnp.concatenate([jnp.where(lane4 == q, half_a, 0.0) for q in range(4)], 0)
        for half in range(2):
            head_ref[slot, half] = jnp.concatenate(
                [radial, cols[:, half * HID : (half + 1) * HID], jnp.concatenate([ident] * 4, 0)], 1
            ).astype(BF16)
        adds_ref[slot] = jnp.concatenate([0.5 * proj_b] * 2, 1).astype(BF16)
        turned_ref[slot] = jnp.concatenate([pos_a, live_a, jnp.zeros((CL - 4, CL), F32)], 0).T
        across_ref[slot] = jnp.concatenate([pos_b, live_b, jnp.zeros((4, CL), F32)], 0)
        blocks_ref[slot] = (jnp.minimum(fill_left, fill_right) + ROWS - 1) // ROWS
        return carry

    lax.fori_loop(0, count, prepare, 0)

    def distances(mine, across):
        delta = [mine[:, c : c + 1] - across[c : c + 1] for c in range(3)]
        dist = jnp.sqrt(delta[0] * delta[0] + delta[1] * delta[1] + delta[2] * delta[2] + SOFT)
        return delta, dist

    def enter(slot, g):
        start = pl.multiple_of(g * ROWS, ROWS)
        mine = turned_ref[slot, pl.ds(start, ROWS), :]
        scaled = distances(mine, across_ref[slot])[1] * SCALE
        for e in range(ROWS // 8):
            bases = []
            rates = []
            for q in range(4):
                r = 8 * e + q
                row = jnp.concatenate([scaled[r : r + 1], scaled[r + 4 : r + 5]], 1)
                offset = row - centers
                basis = jnp.exp2(-(offset * offset))
                bases.append(basis.astype(BF16))
                rates.append((basis * offset).astype(BF16))
            block = g * (ROWS // 8) + e
            tail = jnp.concatenate(bases + [pick_ref[block % 8], adds_ref[slot]], 0)
            half1_ref[e] = jnp.dot(head_ref[slot, block // 8], tail, preferred_element_type=F32)
            rate_ref[e] = jnp.dot(
                tangent_ref[...], jnp.concatenate(rates, 0), preferred_element_type=F32
            )

    def middle():
        for e in range(ROWS // 8):
            half1 = half1_ref[e]
            up1 = 1.0 + jnp.tanh(half1)
            silu1 = half1 * up1
            grad1 = up1 + silu1 * (2.0 - up1)
            chain_ref[e] = grad1 * rate_ref[e]
            half2_ref[e] = jnp.dot(hidden_ref[...], silu1.astype(BF16), preferred_element_type=F32)

    def leave(slot, g):
        for e in range(ROWS // 8):
            half2 = half2_ref[e]
            up2 = 1.0 + jnp.tanh(half2)
            silu2 = half2 * up2
            grad2 = up2 + silu2 * (2.0 - up2)
            back1 = jnp.dot(back_ref[...], (half_out * grad2).astype(BF16), preferred_element_type=F32)
            energy = jnp.dot(out_ref[...], silu2.astype(BF16), preferred_element_type=F32)
            terms = back1 * chain_ref[e]
            lines = jnp.concatenate(
                [jnp.sum(terms[q * HID : (q + 1) * HID], 0, keepdims=True) for q in range(4)], 0
            )
            at = pl.ds(pl.multiple_of(g * ROWS + 8 * e, 8), 8)
            slopes_ref[slot, at, :] = jnp.concatenate([lines[:, :CL], lines[:, CL:]], 0)
            energies_ref[slot, at, :] = jnp.concatenate([energy[:4, :CL], energy[:4, CL:]], 0)

    spare = slopes_ref.shape[0] - 1

    def step(carry):
        slot, g, slot1, g1, slot2, g2, left = carry
        leave(slot2, g2)
        middle()
        enter(slot, g)
        last = g + 1 >= blocks_ref[slot]
        ended = jnp.logical_and(last, slot + 1 >= count)
        slot2, g2 = slot1, g1
        slot1 = jnp.where(left > 2, slot, spare)
        g1 = g
        g = jnp.where(ended, g, jnp.where(last, 0, g + 1))
        slot = jnp.where(jnp.logical_and(last, jnp.logical_not(ended)), slot + 1, slot)
        return slot, g, slot1, g1, slot2, g2, left - 1

    total = lax.fori_loop(0, count, lambda slot, n: n + blocks_ref[slot], 0)
    zero = jnp.int32(0)
    far = jnp.int32(spare)
    lax.while_loop(
        lambda carry: carry[6] > 0, step, (zero, zero, far, zero, far, zero, total + 2)
    )

    sub = lax.broadcasted_iota(jnp.int32, (CL, CL), 0)
    lane = lax.broadcasted_iota(jnp.int32, (CL, CL), 1)
    row8 = lax.broadcasted_iota(jnp.int32, (8, CL), 0) // 4

    def finish(slot, carry):
        first = tiles_ref[0, slot]
        other = tiles_ref[1, slot]
        same = base_ref[0] + first == (other // CPD * base_ref[2] + base_ref[1]) * CPD + other % CPD
        mine = turned_ref[slot]
        across = across_ref[slot]
        delta, dist = distances(mine, across)
        mask = mine[:, 3:4] * across[3:4]
        keep = jnp.logical_and(mask > 0.0, jnp.logical_or(jnp.logical_not(same), sub != lane))
        weight = jnp.where(keep, slopes_ref[slot] / dist, 0.0)
        pulls = [weight * d for d in delta]
        parts = [-jnp.sum(p, 1, keepdims=True) for p in pulls]
        kept = jnp.where(keep, energies_ref[slot], 0.0)
        parts.append(jnp.sum(kept, 1, keepdims=True))
        side = jnp.zeros((CL, CL), F32)
        for c in range(4):
            side = jnp.where(lane == c, parts[c], side)
        down = side.T[:4]
        along = jnp.concatenate([jnp.sum(p, 0, keepdims=True) for p in pulls + [kept]], 0)
        swap = swaps_ref[slot] == 1
        firsts = jnp.where(swap, along, down)
        seconds = jnp.where(swap, down, along)
        away = jnp.bitwise_xor(first // CPD, base_ref[1])
        first_ref[away % 4 * 4 + away // 4] += jnp.where(row8 == first % CPD, jnp.concatenate([firsts] * 2, 0), 0.0)
        second_ref[other // CPD] += jnp.where(
            row8 == other % CPD, jnp.concatenate([seconds] * 2, 0), 0.0
        )
        return carry

    lax.fori_loop(0, count, finish, 0)


def tile_call(tiles, tile_count, base, left, right, w_radial, w_hidden, w_out):
    smem = pl.BlockSpec(memory_space=pltpu.SMEM)
    vmem = pl.BlockSpec(memory_space=pltpu.VMEM)
    slots = tiles.shape[0]
    groups = ROWS // 8
    hid4 = 4 * HID
    wide = 2 * CL
    return pl.pallas_call(
        tile_kernel,
        name="tiles",
        out_shape=(
            jax.ShapeDtypeStruct((left.shape[0] // CPD, 8, CL), F32),
            jax.ShapeDtypeStruct((right.shape[0] // CPD, 8, CL), F32),
        ),
        in_specs=[smem] * 3 + [vmem] * 5,
        out_specs=(vmem, vmem),
        scratch_shapes=[
            pltpu.VMEM((hid4, 4 * NRBF), BF16),
            pltpu.VMEM((hid4, hid4), BF16),
            pltpu.VMEM((hid4, hid4), BF16),
            pltpu.VMEM((8, hid4), BF16),
            pltpu.VMEM((HID // 8, HID, wide), BF16),
            pltpu.VMEM((slots, 2, hid4, hid4), BF16),
            pltpu.VMEM((slots, HID, wide), BF16),
            pltpu.VMEM((slots, CL, CL), F32),
            pltpu.VMEM((slots, 8, CL), F32),
            pltpu.VMEM((slots + 1, CL, CL), F32),
            pltpu.VMEM((slots + 1, CL, CL), F32),
            pltpu.VMEM((groups, hid4, wide), F32),
            pltpu.VMEM((groups, hid4, wide), F32),
            pltpu.VMEM((groups, hid4, wide), F32),
            pltpu.VMEM((groups, hid4, wide), F32),
            pltpu.SMEM((slots,), jnp.int32),
            pltpu.SMEM((slots,), jnp.int32),
        ],
        compiler_params=pltpu.CompilerParams(vmem_limit_bytes=48 * 1024 * 1024),
    )(
        tiles.T, tile_count, base, left, right, w_radial.T, w_hidden, w_out.astype(F32)[:, None],
    )


def across(count, step):
    return [(i, i ^ step) for i in range(count)]


def add_kernel(own_ref, one_ref, two_ref, three_ref, second_ref, force_ref, energy_ref):
    total = own_ref[...] + one_ref[...] + two_ref[...] + three_ref[...]
    other = second_ref[0]
    for peer in range(1, second_ref.shape[0]):
        other = other + second_ref[peer]
    force = total + other
    for k in range(CPD):
        cut = slice(k * CL, (k + 1) * CL)
        force_ref[:, cut] = force[4 * k : 4 * k + 3]
        energy_ref[:, cut] = total[4 * k + 3 : 4 * k + 4]


def body(positions, features, fill, tiles, tile_count, w_radial, w_left, w_right, w_hidden, w_out):
    rows = lax.axis_size("row")
    cols = lax.axis_size("col")
    smem = pl.BlockSpec(memory_space=pltpu.SMEM)
    vmem = pl.BlockSpec(memory_space=pltpu.VMEM)
    with jax.named_scope("pack"):
        left, right = pl.pallas_call(
            pack_kernel,
            out_shape=(
                jax.ShapeDtypeStruct((1, CPD, PAY, CL), BF16),
                jax.ShapeDtypeStruct((1, CPD, PAY, CL), BF16),
            ),
            in_specs=[smem] + [vmem] * 4,
            out_specs=(vmem, vmem),
        )(fill, positions, features, w_left.T, w_right.T)
    with jax.named_scope("spread"):
        left, right = [
            jnp.concatenate([own] + [lax.ppermute(own, axis, across(16, k)) for k in range(1, 4)], 0)
            for own, axis in ((left, "col"), (right, "row"))
        ]
        left, right = [
            jnp.concatenate([own] + [lax.ppermute(own, axis, across(16, 4 * k)) for k in range(1, 4)], 0)
            .reshape(16 * CPD, PAY, CL)
            for own, axis in ((left, "col"), (right, "row"))
        ]
    base = jnp.stack(
        [lax.axis_index("row") * cols * CPD, lax.axis_index("col"), jnp.int32(cols), lax.axis_index("row")]
    )
    with jax.named_scope("tiles"):
        firsts, seconds = tile_call(
            tiles, tile_count, base, left, right, w_radial, w_hidden, w_out
        )
    with jax.named_scope("collect"):
        seconds = lax.all_to_all(seconds, "row", 0, 0)
        firsts = firsts.reshape(4, 4, 8, CL)
        near = firsts[0]
        for k in range(1, 4):
            near = near + lax.ppermute(firsts[k], "col", across(cols, k))
        firsts = [near[0]] + [lax.ppermute(near[k], "col", across(cols, 4 * k)) for k in range(1, 4)]
    with jax.named_scope("add"):
        force, energy = pl.pallas_call(
            add_kernel,
            out_shape=(
                jax.ShapeDtypeStruct((3, CPD * CL), F32),
                jax.ShapeDtypeStruct((1, CPD * CL), F32),
            ),
        )(*firsts, seconds)
    return force, energy.reshape(CPD * CL)


def solution(mesh):
    return jax.shard_map(
        body,
        mesh=mesh,
        in_specs=(
            P(None, ("row", "col")),
            P(None, ("row", "col")),
            P(("row", "col")),
            P(("row", "col"), None),
            P(("row", "col")),
            P(),
            P(),
            P(),
            P(),
            P(),
        ),
        out_specs=(P(None, ("row", "col")), P(("row", "col"))),
        check_vma=False,
    )
```

```python
import functools

import jax
import jax.numpy as jnp
from jax import lax
from jax.experimental import pallas as pl
from jax.experimental.pallas import tpu as pltpu
from jax.sharding import PartitionSpec as P

CL = 128
CPD = 2
HID = 64
NRBF = 32
PAY = 80
LIVE = HID + 9
GROUPS = 4
SOFT = 0.01
RANGE = 6.0
SHARP = ((NRBF - 1) / RANGE) ** 2
LOG2E = 1.4426950408889634
SCALE = (SHARP * LOG2E) ** 0.5

F32 = jnp.float32
BF16 = jnp.bfloat16


def pack_kernel(fill_ref, pos_ref, feat_ref, wl_ref, wr_ref, left_ref, right_ref):
    feat = feat_ref[...]
    pos = pos_ref[...]
    high = pos.astype(BF16).astype(F32)
    rest = pos - high
    mid = rest.astype(BF16).astype(F32)
    low = (rest - mid).astype(BF16).astype(F32)
    lane = lax.broadcasted_iota(jnp.int32, (1, CL), 1)
    for weight_ref, out_ref in ((wl_ref, left_ref), (wr_ref, right_ref)):
        proj = jnp.dot(weight_ref[...], feat, preferred_element_type=F32)
        for k in range(CPD):
            cut = slice(k * CL, (k + 1) * CL)
            live = (lane < fill_ref[k]).astype(F32)
            extra = jnp.concatenate(
                [high[:, cut], mid[:, cut], low[:, cut], live, jnp.zeros((6, CL), F32)], 0
            )
            both = jnp.concatenate([proj[:, cut], extra], 0).astype(BF16)
            for peer in range(out_ref.shape[0]):
                out_ref[peer, k] = both


def unpack(block):
    extra = block[HID:]
    pos = extra[0:3] + extra[3:6] + extra[6:9]
    return block[:HID], pos, extra[9:10]


def spread4(value):
    rows, cols = value.shape
    tall = jnp.concatenate([value] * 4, 0)
    wide = jnp.concatenate([tall] * 4, 1)
    down = lax.broadcasted_iota(jnp.int32, wide.shape, 0) // rows
    across = lax.broadcasted_iota(jnp.int32, wide.shape, 1) // cols
    return jnp.where(down == across, wide, 0.0)


def tile_kernel(
    tiles_ref, count_ref, base_ref, left_ref, right_ref, wr_ref, wh_ref, wo_ref,
    first_ref, second_ref,
    tangent_ref, hidden_ref, back_ref, out_ref, pick_ref, head_ref, adds_ref,
    turned_ref, across_ref, slopes_ref, energies_ref, half1_ref, rate_ref, half2_ref, chain_ref, source_ref, target_ref, swaps_ref,
):
    count = count_ref[0]
    wide = 2 * CL
    first_ref[...] = jnp.zeros_like(first_ref)
    second_ref[...] = jnp.zeros_like(second_ref)
    w_radial = wr_ref[...].T
    radial = spread4(0.5 * w_radial)
    tangent = spread4(w_radial * (-SHARP / SCALE))
    high = tangent.astype(BF16).astype(F32)
    tangent_ref[...] = jnp.concatenate([high, tangent - high], 1).astype(BF16)
    w_hidden = wh_ref[...].astype(F32)
    w_out = wo_ref[...]
    hidden_ref[...] = spread4(0.5 * w_hidden).astype(BF16)
    back_ref[...] = spread4(w_hidden.T).astype(BF16)
    half_out = jnp.broadcast_to(jnp.concatenate([0.5 * w_out] * 4, 0), (4 * HID, wide))
    flat_out = jnp.concatenate([w_out.T] * 4, 1)
    lane8 = lax.broadcasted_iota(jnp.int32, (8, 4 * HID), 1) // HID
    sub8 = lax.broadcasted_iota(jnp.int32, (8, 4 * HID), 0)
    out_ref[...] = jnp.where(lane8 == sub8, flat_out, 0.0).astype(BF16)
    quad = lax.broadcasted_iota(jnp.int32, (HID, wide), 0) // 4
    side = lax.broadcasted_iota(jnp.int32, (HID, wide), 1) // CL
    for g in range(HID // 8):
        pick_ref[g] = (quad == 2 * g + side).astype(F32).astype(BF16)
    centers = (
        lax.broadcasted_iota(jnp.int32, (NRBF, wide), 0).astype(F32) * (RANGE / (NRBF - 1) * SCALE)
    )
    ident = (
        lax.broadcasted_iota(jnp.int32, (HID, HID), 0)
        == lax.broadcasted_iota(jnp.int32, (HID, HID), 1)
    ).astype(F32)
    lane4 = lax.broadcasted_iota(jnp.int32, (HID, CL), 1) % 4

    def prepare(slot, carry):
        first = tiles_ref[0, slot]
        away = jnp.bitwise_xor(first // CPD, base_ref[1])
        left = left_ref[away * CPD + first % CPD].astype(F32)
        other = tiles_ref[1, slot]
        beyond = jnp.bitwise_xor(other // CPD, base_ref[3])
        right = right_ref[beyond * CPD + other % CPD].astype(F32)
        fill_left = jnp.sum(left[LIVE : LIVE + 1]).astype(jnp.int32)
        fill_right = jnp.sum(right[LIVE : LIVE + 1]).astype(jnp.int32)
        swap = fill_right < fill_left
        swaps_ref[slot] = swap.astype(jnp.int32)
        proj_a, pos_a, live_a = unpack(jnp.where(swap, right, left))
        proj_b, pos_b, live_b = unpack(jnp.where(swap, left, right))
        half_a = 0.5 * proj_a
        cols = jnp.concatenate([jnp.where(lane4 == q, half_a, 0.0) for q in range(4)], 0)
        for half in range(2):
            head_ref[slot, half] = jnp.concatenate(
                [radial, cols[:, half * HID : (half + 1) * HID], jnp.concatenate([ident] * 4, 0)], 1
            ).astype(BF16)
        adds_ref[slot] = jnp.concatenate([0.5 * proj_b] * 2, 1).astype(BF16)
        turned_ref[slot] = jnp.concatenate([pos_a, live_a, jnp.zeros((CL - 4, CL), F32)], 0).T
        across_ref[slot] = jnp.concatenate([pos_b, live_b, jnp.zeros((4, CL), F32)], 0)
        mine = jnp.where(slot < count, (jnp.minimum(fill_left, fill_right) + 7) // 8, 0)

        def enlist(g, at):
            source_ref[at] = slot * 16 + g
            target_ref[at + 2 * GROUPS] = slot * 16 + g
            return at + 1

        return lax.fori_loop(0, mine, enlist, carry)

    groups = lax.fori_loop(0, tiles_ref.shape[1], prepare, jnp.int32(0), unroll=2)
    spare = slopes_ref.shape[0] - 1
    for k in range(2 * GROUPS):
        target_ref[k] = spare * 16
    for k in range(3 * GROUPS):
        source_ref[groups + k] = 0
        target_ref[groups + 2 * GROUPS + k] = spare * 16

    def distances(mine, across):
        delta = [mine[:, c : c + 1] - across[c : c + 1] for c in range(3)]
        dist = jnp.sqrt(delta[0] * delta[0] + delta[1] * delta[1] + delta[2] * delta[2] + SOFT)
        return delta, dist

    def place(list_ref, at):
        return list_ref[at] // 16, list_ref[at] % 16

    def enter(n):
        for e in range(GROUPS):
            slot, g = place(source_ref, n * GROUPS + e)
            mine = turned_ref[slot, pl.ds(pl.multiple_of(g * 8, 8), 8), :]
            scaled = distances(mine, across_ref[slot])[1] * SCALE
            bases = []
            rates = []
            for q in range(4):
                row = jnp.concatenate([scaled[q : q + 1], scaled[q + 4 : q + 5]], 1)
                offset = row - centers
                basis = jnp.exp2(-(offset * offset))
                bases.append(basis.astype(BF16))
                rates.append((basis * offset).astype(BF16))
            tail = jnp.concatenate(bases + [pick_ref[g % 8], adds_ref[slot]], 0)
            half1_ref[e] = jnp.dot(head_ref[slot, g // 8], tail, preferred_element_type=F32)
            rate_ref[e] = jnp.dot(
                tangent_ref[...], jnp.concatenate(rates + rates, 0), preferred_element_type=F32
            )

    def middle():
        for e in range(GROUPS):
            half1 = half1_ref[e]
            up1 = 1.0 + jnp.tanh(half1)
            silu1 = half1 * up1
            grad1 = up1 + silu1 * (2.0 - up1)
            chain_ref[e] = grad1 * rate_ref[e]
            half2_ref[e] = jnp.dot(hidden_ref[...], silu1.astype(BF16), preferred_element_type=F32)

    def leave(n):
        for e in range(GROUPS):
            slot, g = place(target_ref, n * GROUPS + e)
            half2 = half2_ref[e]
            up2 = 1.0 + jnp.tanh(half2)
            silu2 = half2 * up2
            grad2 = up2 + silu2 * (2.0 - up2)
            back1 = jnp.dot(back_ref[...], (half_out * grad2).astype(BF16), preferred_element_type=F32)
            energy = jnp.dot(out_ref[...], silu2.astype(BF16), preferred_element_type=F32)
            terms = back1 * chain_ref[e]
            lines = jnp.concatenate(
                [jnp.sum(terms[q * HID : (q + 1) * HID], 0, keepdims=True) for q in range(4)], 0
            )
            at = pl.ds(pl.multiple_of(g * 8, 8), 8)
            slopes_ref[slot, at, :] = jnp.concatenate([lines[:, :CL], lines[:, CL:]], 0)
            energies_ref[slot, at, :] = jnp.concatenate([energy[:4, :CL], energy[:4, CL:]], 0)

    def step(n, carry):
        leave(n)
        middle()
        enter(n)
        return carry

    lax.fori_loop(0, (groups + GROUPS - 1) // GROUPS + 2, step, 0)

    sub = lax.broadcasted_iota(jnp.int32, (CL, CL), 0)
    lane = lax.broadcasted_iota(jnp.int32, (CL, CL), 1)
    row8 = lax.broadcasted_iota(jnp.int32, (8, CL), 0) // 4

    def finish(slot, carry):
        first = tiles_ref[0, slot]
        other = tiles_ref[1, slot]
        same = base_ref[0] + first == (other // CPD * base_ref[2] + base_ref[1]) * CPD + other % CPD
        mine = turned_ref[slot]
        across = across_ref[slot]
        delta, dist = distances(mine, across)
        mask = mine[:, 3:4] * across[3:4] * (slot < count).astype(F32)
        keep = jnp.logical_and(mask > 0.0, jnp.logical_or(jnp.logical_not(same), sub != lane))
        weight = jnp.where(keep, slopes_ref[slot] / dist, 0.0)
        pulls = [weight * d for d in delta]
        parts = [-jnp.sum(p, 1, keepdims=True) for p in pulls]
        kept = jnp.where(keep, energies_ref[slot], 0.0)
        parts.append(jnp.sum(kept, 1, keepdims=True))
        side = jnp.zeros((CL, CL), F32)
        for c in range(4):
            side = jnp.where(lane == c, parts[c], side)
        down = side.T[:4]
        along = jnp.concatenate([jnp.sum(p, 0, keepdims=True) for p in pulls + [kept]], 0)
        swap = swaps_ref[slot] == 1
        firsts = jnp.where(swap, along, down)
        seconds = jnp.where(swap, down, along)
        away = jnp.bitwise_xor(first // CPD, base_ref[1])
        first_ref[away % 4 * 4 + away // 4] += jnp.where(row8 == first % CPD, jnp.concatenate([firsts] * 2, 0), 0.0)
        second_ref[other // CPD] += jnp.where(
            row8 == other % CPD, jnp.concatenate([seconds] * 2, 0), 0.0
        )
        return carry

    lax.fori_loop(0, tiles_ref.shape[1], finish, 0, unroll=2)


def tile_call(tiles, tile_count, base, left, right, w_radial, w_hidden, w_out):
    smem = pl.BlockSpec(memory_space=pltpu.SMEM)
    vmem = pl.BlockSpec(memory_space=pltpu.VMEM)
    slots = tiles.shape[0]
    groups = GROUPS
    listed = slots * (CL // 8) + 5 * GROUPS
    hid4 = 4 * HID
    wide = 2 * CL
    return pl.pallas_call(
        tile_kernel,
        name="tiles",
        out_shape=(
            jax.ShapeDtypeStruct((left.shape[0] // CPD, 8, CL), F32),
            jax.ShapeDtypeStruct((right.shape[0] // CPD, 8, CL), F32),
        ),
        in_specs=[smem] * 3 + [vmem] * 5,
        out_specs=(vmem, vmem),
        scratch_shapes=[
            pltpu.VMEM((hid4, 8 * NRBF), BF16),
            pltpu.VMEM((hid4, hid4), BF16),
            pltpu.VMEM((hid4, hid4), BF16),
            pltpu.VMEM((8, hid4), BF16),
            pltpu.VMEM((HID // 8, HID, wide), BF16),
            pltpu.VMEM((slots, 2, hid4, hid4), BF16),
            pltpu.VMEM((slots, HID, wide), BF16),
            pltpu.VMEM((slots, CL, CL), F32),
            pltpu.VMEM((slots, 8, CL), F32),
            pltpu.VMEM((slots + 1, CL, CL), F32),
            pltpu.VMEM((slots + 1, CL, CL), F32),
            pltpu.VMEM((groups, hid4, wide), F32),
            pltpu.VMEM((groups, hid4, wide), F32),
            pltpu.VMEM((groups, hid4, wide), F32),
            pltpu.VMEM((groups, hid4, wide), F32),
            pltpu.SMEM((listed,), jnp.int32),
            pltpu.SMEM((listed,), jnp.int32),
            pltpu.SMEM((slots,), jnp.int32),
        ],
        compiler_params=pltpu.CompilerParams(vmem_limit_bytes=48 * 1024 * 1024),
    )(
        tiles.T, tile_count, base, left, right, w_radial.T, w_hidden, w_out.astype(F32)[:, None],
    )


def across(count, step):
    return [(i, i ^ step) for i in range(count)]


def add_kernel(own_ref, one_ref, two_ref, three_ref, second_ref, force_ref, energy_ref):
    total = own_ref[...] + one_ref[...] + two_ref[...] + three_ref[...]
    other = second_ref[0]
    for peer in range(1, second_ref.shape[0]):
        other = other + second_ref[peer]
    force = total + other
    for k in range(CPD):
        cut = slice(k * CL, (k + 1) * CL)
        force_ref[:, cut] = force[4 * k : 4 * k + 3]
        energy_ref[:, cut] = total[4 * k + 3 : 4 * k + 4]


def body(positions, features, fill, tiles, tile_count, w_radial, w_left, w_right, w_hidden, w_out):
    rows = lax.axis_size("row")
    cols = lax.axis_size("col")
    smem = pl.BlockSpec(memory_space=pltpu.SMEM)
    vmem = pl.BlockSpec(memory_space=pltpu.VMEM)
    with jax.named_scope("pack"):
        left, right = pl.pallas_call(
            pack_kernel,
            out_shape=(
                jax.ShapeDtypeStruct((1, CPD, PAY, CL), BF16),
                jax.ShapeDtypeStruct((1, CPD, PAY, CL), BF16),
            ),
            in_specs=[smem] + [vmem] * 4,
            out_specs=(vmem, vmem),
        )(fill, positions, features, w_left.T, w_right.T)
    with jax.named_scope("spread"):
        left, right = [
            jnp.concatenate([own] + [lax.ppermute(own, axis, across(16, k)) for k in range(1, 4)], 0)
            for own, axis in ((left, "col"), (right, "row"))
        ]
        left, right = [
            jnp.concatenate([own] + [lax.ppermute(own, axis, across(16, 4 * k)) for k in range(1, 4)], 0)
            .reshape(16 * CPD, PAY, CL)
            for own, axis in ((left, "col"), (right, "row"))
        ]
    base = jnp.stack(
        [lax.axis_index("row") * cols * CPD, lax.axis_index("col"), jnp.int32(cols), lax.axis_index("row")]
    )
    with jax.named_scope("tiles"):
        firsts, seconds = tile_call(
            tiles, tile_count, base, left, right, w_radial, w_hidden, w_out
        )
    with jax.named_scope("collect"):
        seconds = lax.all_to_all(seconds, "row", 0, 0)
        firsts = firsts.reshape(4, 4, 8, CL)
        near = firsts[0]
        for k in range(1, 4):
            near = near + lax.ppermute(firsts[k], "col", across(cols, k))
        firsts = [near[0]] + [lax.ppermute(near[k], "col", across(cols, 4 * k)) for k in range(1, 4)]
    with jax.named_scope("add"):
        force, energy = pl.pallas_call(
            add_kernel,
            out_shape=(
                jax.ShapeDtypeStruct((3, CPD * CL), F32),
                jax.ShapeDtypeStruct((1, CPD * CL), F32),
            ),
        )(*firsts, seconds)
    return force, energy.reshape(CPD * CL)


def solution(mesh):
    return jax.shard_map(
        body,
        mesh=mesh,
        in_specs=(
            P(None, ("row", "col")),
            P(None, ("row", "col")),
            P(("row", "col")),
            P(("row", "col"), None),
            P(("row", "col")),
            P(),
            P(),
            P(),
            P(),
            P(),
        ),
        out_specs=(P(None, ("row", "col")), P(("row", "col"))),
        check_vma=False,
    )
```

```python
import functools

import jax
import jax.numpy as jnp
from jax import lax
from jax.experimental import pallas as pl
from jax.experimental.pallas import tpu as pltpu
from jax.sharding import PartitionSpec as P

CL = 128
CPD = 2
HID = 64
NRBF = 32
PAY = 80
LIVE = HID + 9
GROUPS = 4
SOFT = 0.01
RANGE = 6.0
SHARP = ((NRBF - 1) / RANGE) ** 2
LOG2E = 1.4426950408889634
SCALE = (SHARP * LOG2E) ** 0.5

F32 = jnp.float32
BF16 = jnp.bfloat16


def pack_kernel(fill_ref, pos_ref, feat_ref, wl_ref, wr_ref, left_ref, right_ref):
    feat = feat_ref[...]
    pos = pos_ref[...]
    high = pos.astype(BF16).astype(F32)
    rest = pos - high
    mid = rest.astype(BF16).astype(F32)
    low = (rest - mid).astype(BF16).astype(F32)
    lane = lax.broadcasted_iota(jnp.int32, (1, CL), 1)
    for weight_ref, out_ref in ((wl_ref, left_ref), (wr_ref, right_ref)):
        proj = jnp.dot(weight_ref[...], feat, preferred_element_type=F32)
        for k in range(CPD):
            cut = slice(k * CL, (k + 1) * CL)
            live = (lane < fill_ref[k]).astype(F32)
            extra = jnp.concatenate(
                [high[:, cut], mid[:, cut], low[:, cut], live, jnp.zeros((6, CL), F32)], 0
            )
            both = jnp.concatenate([proj[:, cut], extra], 0).astype(BF16)
            for peer in range(out_ref.shape[0]):
                out_ref[peer, k] = both


def unpack(block):
    extra = block[HID:]
    pos = extra[0:3] + extra[3:6] + extra[6:9]
    return block[:HID], pos, extra[9:10]


def spread4(value):
    rows, cols = value.shape
    tall = jnp.concatenate([value] * 4, 0)
    wide = jnp.concatenate([tall] * 4, 1)
    down = lax.broadcasted_iota(jnp.int32, wide.shape, 0) // rows
    across = lax.broadcasted_iota(jnp.int32, wide.shape, 1) // cols
    return jnp.where(down == across, wide, 0.0)


def tile_kernel(
    tiles_ref, count_ref, base_ref, left_ref, right_ref, wr_ref, wh_ref, wo_ref,
    first_ref, second_ref,
    tangent_ref, hidden_ref, back_ref, out_ref, pick_ref, head_ref, adds_ref,
    turned_ref, across_ref, slopes_ref, energies_ref, half1_ref, rate_ref, half2_ref, chain_ref, source_ref, target_ref, swaps_ref,
):
    count = count_ref[0]
    wide = 2 * CL
    first_ref[...] = jnp.zeros_like(first_ref)
    second_ref[...] = jnp.zeros_like(second_ref)
    w_radial = wr_ref[...].T
    radial = spread4(0.5 * w_radial)
    tangent = spread4(w_radial * (-SHARP / SCALE))
    high = tangent.astype(BF16).astype(F32)
    tangent_ref[...] = jnp.concatenate([high, tangent - high], 1).astype(BF16)
    w_hidden = wh_ref[...].astype(F32)
    w_out = wo_ref[...]
    hidden_ref[...] = spread4(0.5 * w_hidden).astype(BF16)
    back_ref[...] = spread4(w_hidden.T).astype(BF16)
    half_out = jnp.broadcast_to(jnp.concatenate([0.5 * w_out] * 4, 0), (4 * HID, wide))
    flat_out = jnp.concatenate([w_out.T] * 4, 1)
    lane8 = lax.broadcasted_iota(jnp.int32, (8, 4 * HID), 1) // HID
    sub8 = lax.broadcasted_iota(jnp.int32, (8, 4 * HID), 0)
    out_ref[...] = jnp.where(lane8 == sub8, flat_out, 0.0).astype(BF16)
    quad = lax.broadcasted_iota(jnp.int32, (HID, wide), 0) // 4
    side = lax.broadcasted_iota(jnp.int32, (HID, wide), 1) // CL
    for g in range(HID // 8):
        pick_ref[g] = (quad == 2 * g + side).astype(F32).astype(BF16)
    centers = (
        lax.broadcasted_iota(jnp.int32, (NRBF, wide), 0).astype(F32) * (RANGE / (NRBF - 1) * SCALE)
    )
    ident = (
        lax.broadcasted_iota(jnp.int32, (HID, HID), 0)
        == lax.broadcasted_iota(jnp.int32, (HID, HID), 1)
    ).astype(F32)
    lane4 = lax.broadcasted_iota(jnp.int32, (HID, CL), 1) % 4

    def prepare(slot, carry):
        first = tiles_ref[0, slot]
        away = jnp.bitwise_xor(first // CPD, base_ref[1])
        left = left_ref[away * CPD + first % CPD].astype(F32)
        other = tiles_ref[1, slot]
        beyond = jnp.bitwise_xor(other // CPD, base_ref[3])
        right = right_ref[beyond * CPD + other % CPD].astype(F32)
        fill_left = jnp.sum(left[LIVE : LIVE + 1]).astype(jnp.int32)
        fill_right = jnp.sum(right[LIVE : LIVE + 1]).astype(jnp.int32)
        swap = fill_right < fill_left
        swaps_ref[slot] = swap.astype(jnp.int32)
        proj_a, pos_a, live_a = unpack(jnp.where(swap, right, left))
        proj_b, pos_b, live_b = unpack(jnp.where(swap, left, right))
        half_a = 0.5 * proj_a
        cols = jnp.concatenate([jnp.where(lane4 == q, half_a, 0.0) for q in range(4)], 0)
        for half in range(2):
            head_ref[slot, half] = jnp.concatenate(
                [radial, cols[:, half * HID : (half + 1) * HID], jnp.concatenate([ident] * 4, 0)], 1
            ).astype(BF16)
        adds_ref[slot] = jnp.concatenate([0.5 * proj_b] * 2, 1).astype(BF16)
        turned_ref[slot] = jnp.concatenate([pos_a, live_a, jnp.zeros((CL - 4, CL), F32)], 0).T
        across_ref[slot] = jnp.concatenate([pos_b, live_b, jnp.zeros((4, CL), F32)], 0)
        mine = jnp.where(slot < count, (jnp.minimum(fill_left, fill_right) + 7) // 8, 0)

        def enlist(g, at):
            source_ref[at] = slot * 16 + g
            target_ref[at + 2 * GROUPS] = slot * 16 + g
            return at + 1

        return lax.fori_loop(0, mine, enlist, carry)

    groups = lax.fori_loop(0, tiles_ref.shape[1], prepare, jnp.int32(0), unroll=2)
    spare = slopes_ref.shape[0] - 1
    for k in range(2 * GROUPS):
        target_ref[k] = spare * 16
    for k in range(3 * GROUPS):
        source_ref[groups + k] = 0
        target_ref[groups + 2 * GROUPS + k] = spare * 16

    def distances(mine, across):
        delta = [mine[:, c : c + 1] - across[c : c + 1] for c in range(3)]
        dist = jnp.sqrt(delta[0] * delta[0] + delta[1] * delta[1] + delta[2] * delta[2] + SOFT)
        return delta, dist

    def place(list_ref, at):
        return list_ref[at] // 16, list_ref[at] % 16

    def enter(n):
        for e in range(GROUPS):
            slot, g = place(source_ref, n * GROUPS + e)
            mine = turned_ref[slot, pl.ds(pl.multiple_of(g * 8, 8), 8), :]
            scaled = distances(mine, across_ref[slot])[1] * SCALE
            bases = []
            rates = []
            for q in range(4):
                row = jnp.concatenate([scaled[q : q + 1], scaled[q + 4 : q + 5]], 1)
                offset = row - centers
                basis = jnp.exp2(-(offset * offset))
                bases.append(basis.astype(BF16))
                rates.append((basis * offset).astype(BF16))
            tail = jnp.concatenate(bases + [pick_ref[g % 8], adds_ref[slot]], 0)
            half1_ref[e] = jnp.dot(head_ref[slot, g // 8], tail, preferred_element_type=F32)
            rate_ref[e] = jnp.dot(
                tangent_ref[...], jnp.concatenate(rates + rates, 0), preferred_element_type=F32
            )

    def middle():
        for e in range(GROUPS):
            half1 = half1_ref[e]
            up1 = 1.0 + jnp.tanh(half1)
            silu1 = half1 * up1
            grad1 = up1 + silu1 * (2.0 - up1)
            chain_ref[e] = grad1 * rate_ref[e]
            half2_ref[e] = jnp.dot(hidden_ref[...], silu1.astype(BF16), preferred_element_type=F32)

    def leave(n):
        for e in range(GROUPS):
            slot, g = place(target_ref, n * GROUPS + e)
            half2 = half2_ref[e]
            up2 = 1.0 + jnp.tanh(half2)
            silu2 = half2 * up2
            grad2 = up2 + silu2 * (2.0 - up2)
            back1 = jnp.dot(back_ref[...], (half_out * grad2).astype(BF16), preferred_element_type=F32)
            energy = jnp.dot(out_ref[...], silu2.astype(BF16), preferred_element_type=F32)
            terms = back1 * chain_ref[e]
            lines = jnp.concatenate(
                [jnp.sum(terms[q * HID : (q + 1) * HID], 0, keepdims=True) for q in range(4)], 0
            )
            at = pl.ds(pl.multiple_of(g * 8, 8), 8)
            slopes_ref[slot, at, :] = jnp.concatenate([lines[:, :CL], lines[:, CL:]], 0)
            energies_ref[slot, at, :] = jnp.concatenate([energy[:4, :CL], energy[:4, CL:]], 0)

    def step(n, carry):
        leave(n)
        middle()
        enter(n)
        return carry

    steps = (groups + GROUPS - 1) // GROUPS
    enter(0)
    middle()
    enter(1)
    lax.fori_loop(2, steps, step, 0)
    leave(steps)
    middle()
    leave(steps + 1)

    sub = lax.broadcasted_iota(jnp.int32, (CL, CL), 0)
    lane = lax.broadcasted_iota(jnp.int32, (CL, CL), 1)
    row8 = lax.broadcasted_iota(jnp.int32, (8, CL), 0) // 4

    def finish(slot, carry):
        first = tiles_ref[0, slot]
        other = tiles_ref[1, slot]
        same = base_ref[0] + first == (other // CPD * base_ref[2] + base_ref[1]) * CPD + other % CPD
        mine = turned_ref[slot]
        across = across_ref[slot]
        delta, dist = distances(mine, across)
        mask = mine[:, 3:4] * across[3:4] * (slot < count).astype(F32)
        keep = jnp.logical_and(mask > 0.0, jnp.logical_or(jnp.logical_not(same), sub != lane))
        weight = jnp.where(keep, slopes_ref[slot] / dist, 0.0)
        pulls = [weight * d for d in delta]
        kept = jnp.where(keep, energies_ref[slot], 0.0)
        down = jnp.concatenate(
            [-jnp.sum(p.T, 0, keepdims=True) for p in pulls] + [jnp.sum(kept.T, 0, keepdims=True)], 0
        )
        along = jnp.concatenate([jnp.sum(p, 0, keepdims=True) for p in pulls + [kept]], 0)
        swap = swaps_ref[slot] == 1
        firsts = jnp.where(swap, along, down)
        seconds = jnp.where(swap, down, along)
        away = jnp.bitwise_xor(first // CPD, base_ref[1])
        first_ref[away % 4 * 4 + away // 4] += jnp.where(row8 == first % CPD, jnp.concatenate([firsts] * 2, 0), 0.0)
        second_ref[other // CPD] += jnp.where(
            row8 == other % CPD, jnp.concatenate([seconds] * 2, 0), 0.0
        )
        return carry

    for slot in range(tiles_ref.shape[1]):
        finish(slot, 0)


def tile_call(tiles, tile_count, base, left, right, w_radial, w_hidden, w_out):
    smem = pl.BlockSpec(memory_space=pltpu.SMEM)
    vmem = pl.BlockSpec(memory_space=pltpu.VMEM)
    slots = tiles.shape[0]
    groups = GROUPS
    listed = slots * (CL // 8) + 5 * GROUPS
    hid4 = 4 * HID
    wide = 2 * CL
    return pl.pallas_call(
        tile_kernel,
        name="tiles",
        out_shape=(
            jax.ShapeDtypeStruct((left.shape[0] // CPD, 8, CL), F32),
            jax.ShapeDtypeStruct((right.shape[0] // CPD, 8, CL), F32),
        ),
        in_specs=[smem] * 3 + [vmem] * 5,
        out_specs=(vmem, vmem),
        scratch_shapes=[
            pltpu.VMEM((hid4, 8 * NRBF), BF16),
            pltpu.VMEM((hid4, hid4), BF16),
            pltpu.VMEM((hid4, hid4), BF16),
            pltpu.VMEM((8, hid4), BF16),
            pltpu.VMEM((HID // 8, HID, wide), BF16),
            pltpu.VMEM((slots, 2, hid4, hid4), BF16),
            pltpu.VMEM((slots, HID, wide), BF16),
            pltpu.VMEM((slots, CL, CL), F32),
            pltpu.VMEM((slots, 8, CL), F32),
            pltpu.VMEM((slots + 1, CL, CL), F32),
            pltpu.VMEM((slots + 1, CL, CL), F32),
            pltpu.VMEM((groups, hid4, wide), F32),
            pltpu.VMEM((groups, hid4, wide), F32),
            pltpu.VMEM((groups, hid4, wide), F32),
            pltpu.VMEM((groups, hid4, wide), F32),
            pltpu.SMEM((listed,), jnp.int32),
            pltpu.SMEM((listed,), jnp.int32),
            pltpu.SMEM((slots,), jnp.int32),
        ],
        compiler_params=pltpu.CompilerParams(vmem_limit_bytes=48 * 1024 * 1024),
    )(
        tiles.T, tile_count, base, left, right, w_radial.T, w_hidden, w_out.astype(F32)[:, None],
    )


def across(count, step):
    return [(i, i ^ step) for i in range(count)]


def add_kernel(own_ref, one_ref, two_ref, three_ref, second_ref, force_ref, energy_ref):
    total = own_ref[...] + one_ref[...] + two_ref[...] + three_ref[...]
    other = second_ref[0]
    for peer in range(1, second_ref.shape[0]):
        other = other + second_ref[peer]
    force = total + other
    for k in range(CPD):
        cut = slice(k * CL, (k + 1) * CL)
        force_ref[:, cut] = force[4 * k : 4 * k + 3]
        energy_ref[:, cut] = total[4 * k + 3 : 4 * k + 4]


def body(positions, features, fill, tiles, tile_count, w_radial, w_left, w_right, w_hidden, w_out):
    rows = lax.axis_size("row")
    cols = lax.axis_size("col")
    smem = pl.BlockSpec(memory_space=pltpu.SMEM)
    vmem = pl.BlockSpec(memory_space=pltpu.VMEM)
    with jax.named_scope("pack"):
        left, right = pl.pallas_call(
            pack_kernel,
            out_shape=(
                jax.ShapeDtypeStruct((1, CPD, PAY, CL), BF16),
                jax.ShapeDtypeStruct((1, CPD, PAY, CL), BF16),
            ),
            in_specs=[smem] + [vmem] * 4,
            out_specs=(vmem, vmem),
        )(fill, positions, features, w_left.T, w_right.T)
    with jax.named_scope("spread"):
        left, right = [
            jnp.concatenate([own] + [lax.ppermute(own, axis, across(16, k)) for k in range(1, 4)], 0)
            for own, axis in ((left, "col"), (right, "row"))
        ]
        left, right = [
            jnp.concatenate([own] + [lax.ppermute(own, axis, across(16, 4 * k)) for k in range(1, 4)], 0)
            .reshape(16 * CPD, PAY, CL)
            for own, axis in ((left, "col"), (right, "row"))
        ]
    base = jnp.stack(
        [lax.axis_index("row") * cols * CPD, lax.axis_index("col"), jnp.int32(cols), lax.axis_index("row")]
    )
    with jax.named_scope("tiles"):
        firsts, seconds = tile_call(
            tiles, tile_count, base, left, right, w_radial, w_hidden, w_out
        )
    with jax.named_scope("collect"):
        seconds = lax.all_to_all(seconds, "row", 0, 0)
        firsts = firsts.reshape(4, 4, 8, CL)
        near = firsts[0]
        for k in range(1, 4):
            near = near + lax.ppermute(firsts[k], "col", across(cols, k))
        firsts = [near[0]] + [lax.ppermute(near[k], "col", across(cols, 4 * k)) for k in range(1, 4)]
    with jax.named_scope("add"):
        force, energy = pl.pallas_call(
            add_kernel,
            out_shape=(
                jax.ShapeDtypeStruct((3, CPD * CL), F32),
                jax.ShapeDtypeStruct((1, CPD * CL), F32),
            ),
        )(*firsts, seconds)
    return force, energy.reshape(CPD * CL)


def solution(mesh):
    return jax.shard_map(
        body,
        mesh=mesh,
        in_specs=(
            P(None, ("row", "col")),
            P(None, ("row", "col")),
            P(("row", "col")),
            P(("row", "col"), None),
            P(("row", "col")),
            P(),
            P(),
            P(),
            P(),
            P(),
        ),
        out_specs=(P(None, ("row", "col")), P(("row", "col"))),
        check_vma=False,
    )
```

```python
import functools

import jax
import jax.numpy as jnp
from jax import lax
from jax.experimental import pallas as pl
from jax.experimental.pallas import tpu as pltpu
from jax.sharding import PartitionSpec as P

CL = 128
CPD = 2
HID = 64
NRBF = 32
PAY = 80
LIVE = HID + 9
GROUPS = 4
SOFT = 0.01
RANGE = 6.0
SHARP = ((NRBF - 1) / RANGE) ** 2
LOG2E = 1.4426950408889634
SCALE = (SHARP * LOG2E) ** 0.5

F32 = jnp.float32
BF16 = jnp.bfloat16


def pack_kernel(fill_ref, pos_ref, feat_ref, wl_ref, wr_ref, left_ref, right_ref):
    feat = feat_ref[...]
    pos = pos_ref[...]
    high = pos.astype(BF16).astype(F32)
    rest = pos - high
    mid = rest.astype(BF16).astype(F32)
    low = (rest - mid).astype(BF16).astype(F32)
    lane = lax.broadcasted_iota(jnp.int32, (1, CL), 1)
    for weight_ref, out_ref in ((wl_ref, left_ref), (wr_ref, right_ref)):
        proj = jnp.dot(weight_ref[...], feat, preferred_element_type=F32)
        for k in range(CPD):
            cut = slice(k * CL, (k + 1) * CL)
            live = (lane < fill_ref[k]).astype(F32)
            extra = jnp.concatenate(
                [high[:, cut], mid[:, cut], low[:, cut], live, jnp.zeros((6, CL), F32)], 0
            )
            both = jnp.concatenate([proj[:, cut], extra], 0).astype(BF16)
            for peer in range(out_ref.shape[0]):
                out_ref[peer, k] = both


def unpack(block):
    extra = block[HID:]
    pos = extra[0:3] + extra[3:6] + extra[6:9]
    return block[:HID], pos, extra[9:10]


def spread4(value):
    rows, cols = value.shape
    tall = jnp.concatenate([value] * 4, 0)
    wide = jnp.concatenate([tall] * 4, 1)
    down = lax.broadcasted_iota(jnp.int32, wide.shape, 0) // rows
    across = lax.broadcasted_iota(jnp.int32, wide.shape, 1) // cols
    return jnp.where(down == across, wide, 0.0)


def tile_kernel(
    tiles_ref, count_ref, base_ref, left_ref, right_ref, wr_ref, wh_ref, wo_ref,
    first_ref, second_ref,
    tangent_ref, hidden_ref, back_ref, out_ref, pick_ref, head_ref, adds_ref,
    turned_ref, across_ref, slopes_ref, energies_ref, half1_ref, rate_ref, half2_ref, chain_ref, source_ref, target_ref, swaps_ref,
):
    count = count_ref[0]
    wide = 2 * CL
    first_ref[...] = jnp.zeros_like(first_ref)
    second_ref[...] = jnp.zeros_like(second_ref)
    w_radial = wr_ref[...].T
    radial = spread4(0.5 * w_radial)
    tangent = spread4(w_radial * (-SHARP / SCALE))
    high = tangent.astype(BF16).astype(F32)
    tangent_ref[...] = jnp.concatenate([high, tangent - high], 1).astype(BF16)
    w_hidden = wh_ref[...].astype(F32)
    w_out = wo_ref[...]
    hidden_ref[...] = spread4(0.5 * w_hidden).astype(BF16)
    back_ref[...] = spread4(w_hidden.T).astype(BF16)
    half_out = jnp.broadcast_to(jnp.concatenate([0.5 * w_out] * 4, 0), (4 * HID, wide))
    flat_out = jnp.concatenate([w_out.T] * 4, 1)
    lane8 = lax.broadcasted_iota(jnp.int32, (8, 4 * HID), 1) // HID
    sub8 = lax.broadcasted_iota(jnp.int32, (8, 4 * HID), 0)
    out_ref[...] = jnp.where(lane8 == sub8, flat_out, 0.0).astype(BF16)
    quad = lax.broadcasted_iota(jnp.int32, (HID, wide), 0) // 4
    side = lax.broadcasted_iota(jnp.int32, (HID, wide), 1) // CL
    for g in range(HID // 8):
        pick_ref[g] = (quad == 2 * g + side).astype(F32).astype(BF16)
    centers = (
        lax.broadcasted_iota(jnp.int32, (NRBF, wide), 0).astype(F32) * (RANGE / (NRBF - 1) * SCALE)
    )
    ident = (
        lax.broadcasted_iota(jnp.int32, (HID, HID), 0)
        == lax.broadcasted_iota(jnp.int32, (HID, HID), 1)
    ).astype(F32)
    lane4 = lax.broadcasted_iota(jnp.int32, (HID, CL), 1) % 4

    def prepare(slot):
        first = tiles_ref[0, slot]
        away = jnp.bitwise_xor(first // CPD, base_ref[1])
        left = left_ref[away * CPD + first % CPD].astype(F32)
        other = tiles_ref[1, slot]
        beyond = jnp.bitwise_xor(other // CPD, base_ref[3])
        right = right_ref[beyond * CPD + other % CPD].astype(F32)
        fill_left = jnp.sum(left[LIVE : LIVE + 1]).astype(jnp.int32)
        fill_right = jnp.sum(right[LIVE : LIVE + 1]).astype(jnp.int32)
        swap = fill_right < fill_left
        swaps_ref[slot] = swap.astype(jnp.int32)
        proj_a, pos_a, live_a = unpack(jnp.where(swap, right, left))
        proj_b, pos_b, live_b = unpack(jnp.where(swap, left, right))
        half_a = 0.5 * proj_a
        cols = jnp.concatenate([jnp.where(lane4 == q, half_a, 0.0) for q in range(4)], 0)
        for half in range(2):
            head_ref[slot, half] = jnp.concatenate(
                [radial, cols[:, half * HID : (half + 1) * HID], jnp.concatenate([ident] * 4, 0)], 1
            ).astype(BF16)
        adds_ref[slot] = jnp.concatenate([0.5 * proj_b] * 2, 1).astype(BF16)
        turned_ref[slot] = jnp.concatenate([pos_a, live_a, jnp.zeros((CL - 4, CL), F32)], 0).T
        across_ref[slot] = jnp.concatenate([pos_b, live_b, jnp.zeros((4, CL), F32)], 0)
        return jnp.where(slot < count, (jnp.minimum(fill_left, fill_right) + 7) // 8, 0)

    sizes = [prepare(slot) for slot in range(tiles_ref.shape[1])]
    groups = jnp.int32(0)
    for slot, size in enumerate(sizes):
        for g in range(CL // 8):
            source_ref[groups + g] = slot * 16 + g
            target_ref[groups + 2 * GROUPS + g] = slot * 16 + g
        groups = groups + size
    spare = slopes_ref.shape[0] - 1
    for k in range(2 * GROUPS):
        target_ref[k] = spare * 16
    for k in range(3 * GROUPS):
        source_ref[groups + k] = 0
        target_ref[groups + 2 * GROUPS + k] = spare * 16

    def distances(mine, across):
        delta = [mine[:, c : c + 1] - across[c : c + 1] for c in range(3)]
        dist = jnp.sqrt(delta[0] * delta[0] + delta[1] * delta[1] + delta[2] * delta[2] + SOFT)
        return delta, dist

    def place(list_ref, at):
        return list_ref[at] // 16, list_ref[at] % 16

    def enter(n):
        for e in range(GROUPS):
            slot, g = place(source_ref, n * GROUPS + e)
            mine = turned_ref[slot, pl.ds(pl.multiple_of(g * 8, 8), 8), :]
            scaled = distances(mine, across_ref[slot])[1] * SCALE
            bases = []
            rates = []
            for q in range(4):
                row = jnp.concatenate([scaled[q : q + 1], scaled[q + 4 : q + 5]], 1)
                offset = row - centers
                basis = jnp.exp2(-(offset * offset))
                bases.append(basis.astype(BF16))
                rates.append((basis * offset).astype(BF16))
            tail = jnp.concatenate(bases + [pick_ref[g % 8], adds_ref[slot]], 0)
            half1_ref[e] = jnp.dot(head_ref[slot, g // 8], tail, preferred_element_type=F32)
            rate_ref[e] = jnp.dot(
                tangent_ref[...], jnp.concatenate(rates + rates, 0), preferred_element_type=F32
            )

    def middle():
        for e in range(GROUPS):
            half1 = half1_ref[e]
            up1 = 1.0 + jnp.tanh(half1)
            silu1 = half1 * up1
            grad1 = up1 + silu1 * (2.0 - up1)
            chain_ref[e] = grad1 * rate_ref[e]
            half2_ref[e] = jnp.dot(hidden_ref[...], silu1.astype(BF16), preferred_element_type=F32)

    def leave(n):
        for e in range(GROUPS):
            slot, g = place(target_ref, n * GROUPS + e)
            half2 = half2_ref[e]
            up2 = 1.0 + jnp.tanh(half2)
            silu2 = half2 * up2
            grad2 = up2 + silu2 * (2.0 - up2)
            back1 = jnp.dot(back_ref[...], (half_out * grad2).astype(BF16), preferred_element_type=F32)
            energy = jnp.dot(out_ref[...], silu2.astype(BF16), preferred_element_type=F32)
            terms = back1 * chain_ref[e]
            lines = jnp.concatenate(
                [jnp.sum(terms[q * HID : (q + 1) * HID], 0, keepdims=True) for q in range(4)], 0
            )
            at = pl.ds(pl.multiple_of(g * 8, 8), 8)
            slopes_ref[slot, at, :] = jnp.concatenate([lines[:, :CL], lines[:, CL:]], 0)
            energies_ref[slot, at, :] = jnp.concatenate([energy[:4, :CL], energy[:4, CL:]], 0)

    def step(n, carry):
        leave(n)
        middle()
        enter(n)
        return carry

    steps = (groups + GROUPS - 1) // GROUPS
    enter(0)
    middle()
    enter(1)
    lax.fori_loop(2, steps, step, 0)
    leave(steps)
    middle()
    leave(steps + 1)

    sub = lax.broadcasted_iota(jnp.int32, (CL, CL), 0)
    lane = lax.broadcasted_iota(jnp.int32, (CL, CL), 1)
    row8 = lax.broadcasted_iota(jnp.int32, (8, CL), 0) // 4

    def finish(slot, carry):
        first = tiles_ref[0, slot]
        other = tiles_ref[1, slot]
        same = base_ref[0] + first == (other // CPD * base_ref[2] + base_ref[1]) * CPD + other % CPD
        mine = turned_ref[slot]
        across = across_ref[slot]
        delta, dist = distances(mine, across)
        mask = mine[:, 3:4] * across[3:4] * (slot < count).astype(F32)
        keep = jnp.logical_and(mask > 0.0, jnp.logical_or(jnp.logical_not(same), sub != lane))
        weight = jnp.where(keep, slopes_ref[slot] / dist, 0.0)
        pulls = [weight * d for d in delta]
        kept = jnp.where(keep, energies_ref[slot], 0.0)
        down = jnp.concatenate(
            [-jnp.sum(p.T, 0, keepdims=True) for p in pulls] + [jnp.sum(kept.T, 0, keepdims=True)], 0
        )
        along = jnp.concatenate([jnp.sum(p, 0, keepdims=True) for p in pulls + [kept]], 0)
        swap = swaps_ref[slot] == 1
        firsts = jnp.where(swap, along, down)
        seconds = jnp.where(swap, down, along)
        away = jnp.bitwise_xor(first // CPD, base_ref[1])
        first_ref[away % 4 * 4 + away // 4] += jnp.where(row8 == first % CPD, jnp.concatenate([firsts] * 2, 0), 0.0)
        second_ref[other // CPD] += jnp.where(
            row8 == other % CPD, jnp.concatenate([seconds] * 2, 0), 0.0
        )
        return carry

    for slot in range(tiles_ref.shape[1]):
        finish(slot, 0)


def tile_call(tiles, tile_count, base, left, right, w_radial, w_hidden, w_out):
    smem = pl.BlockSpec(memory_space=pltpu.SMEM)
    vmem = pl.BlockSpec(memory_space=pltpu.VMEM)
    slots = tiles.shape[0]
    groups = GROUPS
    listed = (slots + 1) * (CL // 8) + 5 * GROUPS
    hid4 = 4 * HID
    wide = 2 * CL
    return pl.pallas_call(
        tile_kernel,
        name="tiles",
        out_shape=(
            jax.ShapeDtypeStruct((left.shape[0] // CPD, 8, CL), F32),
            jax.ShapeDtypeStruct((right.shape[0] // CPD, 8, CL), F32),
        ),
        in_specs=[smem] * 3 + [vmem] * 5,
        out_specs=(vmem, vmem),
        scratch_shapes=[
            pltpu.VMEM((hid4, 8 * NRBF), BF16),
            pltpu.VMEM((hid4, hid4), BF16),
            pltpu.VMEM((hid4, hid4), BF16),
            pltpu.VMEM((8, hid4), BF16),
            pltpu.VMEM((HID // 8, HID, wide), BF16),
            pltpu.VMEM((slots, 2, hid4, hid4), BF16),
            pltpu.VMEM((slots, HID, wide), BF16),
            pltpu.VMEM((slots, CL, CL), F32),
            pltpu.VMEM((slots, 8, CL), F32),
            pltpu.VMEM((slots + 1, CL, CL), F32),
            pltpu.VMEM((slots + 1, CL, CL), F32),
            pltpu.VMEM((groups, hid4, wide), F32),
            pltpu.VMEM((groups, hid4, wide), F32),
            pltpu.VMEM((groups, hid4, wide), F32),
            pltpu.VMEM((groups, hid4, wide), F32),
            pltpu.SMEM((listed,), jnp.int32),
            pltpu.SMEM((listed,), jnp.int32),
            pltpu.SMEM((slots,), jnp.int32),
        ],
        compiler_params=pltpu.CompilerParams(vmem_limit_bytes=48 * 1024 * 1024),
    )(
        tiles.T, tile_count, base, left, right, w_radial.T, w_hidden, w_out.astype(F32)[:, None],
    )


def across(count, step):
    return [(i, i ^ step) for i in range(count)]


def add_kernel(own_ref, one_ref, two_ref, three_ref, second_ref, force_ref, energy_ref):
    total = own_ref[...] + one_ref[...] + two_ref[...] + three_ref[...]
    other = second_ref[0]
    for peer in range(1, second_ref.shape[0]):
        other = other + second_ref[peer]
    force = total + other
    for k in range(CPD):
        cut = slice(k * CL, (k + 1) * CL)
        force_ref[:, cut] = force[4 * k : 4 * k + 3]
        energy_ref[:, cut] = total[4 * k + 3 : 4 * k + 4]


def body(positions, features, fill, tiles, tile_count, w_radial, w_left, w_right, w_hidden, w_out):
    rows = lax.axis_size("row")
    cols = lax.axis_size("col")
    smem = pl.BlockSpec(memory_space=pltpu.SMEM)
    vmem = pl.BlockSpec(memory_space=pltpu.VMEM)
    with jax.named_scope("pack"):
        left, right = pl.pallas_call(
            pack_kernel,
            out_shape=(
                jax.ShapeDtypeStruct((1, CPD, PAY, CL), BF16),
                jax.ShapeDtypeStruct((1, CPD, PAY, CL), BF16),
            ),
            in_specs=[smem] + [vmem] * 4,
            out_specs=(vmem, vmem),
        )(fill, positions, features, w_left.T, w_right.T)
    with jax.named_scope("spread"):
        left, right = [
            jnp.concatenate([own] + [lax.ppermute(own, axis, across(16, k)) for k in range(1, 4)], 0)
            for own, axis in ((left, "col"), (right, "row"))
        ]
        left, right = [
            jnp.concatenate([own] + [lax.ppermute(own, axis, across(16, 4 * k)) for k in range(1, 4)], 0)
            .reshape(16 * CPD, PAY, CL)
            for own, axis in ((left, "col"), (right, "row"))
        ]
    base = jnp.stack(
        [lax.axis_index("row") * cols * CPD, lax.axis_index("col"), jnp.int32(cols), lax.axis_index("row")]
    )
    with jax.named_scope("tiles"):
        firsts, seconds = tile_call(
            tiles, tile_count, base, left, right, w_radial, w_hidden, w_out
        )
    with jax.named_scope("collect"):
        seconds = lax.all_to_all(seconds, "row", 0, 0)
        firsts = firsts.reshape(4, 4, 8, CL)
        near = firsts[0]
        for k in range(1, 4):
            near = near + lax.ppermute(firsts[k], "col", across(cols, k))
        firsts = [near[0]] + [lax.ppermute(near[k], "col", across(cols, 4 * k)) for k in range(1, 4)]
    with jax.named_scope("add"):
        force, energy = pl.pallas_call(
            add_kernel,
            out_shape=(
                jax.ShapeDtypeStruct((3, CPD * CL), F32),
                jax.ShapeDtypeStruct((1, CPD * CL), F32),
            ),
        )(*firsts, seconds)
    return force, energy.reshape(CPD * CL)


def solution(mesh):
    return jax.shard_map(
        body,
        mesh=mesh,
        in_specs=(
            P(None, ("row", "col")),
            P(None, ("row", "col")),
            P(("row", "col")),
            P(("row", "col"), None),
            P(("row", "col")),
            P(),
            P(),
            P(),
            P(),
            P(),
        ),
        out_specs=(P(None, ("row", "col")), P(("row", "col"))),
        check_vma=False,
    )
```

```python
import functools

import jax
import jax.numpy as jnp
from jax import lax
from jax.experimental import pallas as pl
from jax.experimental.pallas import tpu as pltpu
from jax.sharding import PartitionSpec as P

CL = 128
CPD = 2
HID = 64
NRBF = 32
PAY = 72
LIVE = HID + 6
GROUPS = 4
SOFT = 0.01
RANGE = 6.0
SHARP = ((NRBF - 1) / RANGE) ** 2
LOG2E = 1.4426950408889634
SCALE = (SHARP * LOG2E) ** 0.5

F32 = jnp.float32
BF16 = jnp.bfloat16


def pack_kernel(fill_ref, pos_ref, feat_ref, wl_ref, wr_ref, left_ref, right_ref):
    feat = feat_ref[...]
    pos = pos_ref[...]
    high = pos.astype(BF16).astype(F32)
    rest = pos - high
    mid = rest.astype(BF16).astype(F32)
    lane = lax.broadcasted_iota(jnp.int32, (1, CL), 1)
    for weight_ref, out_ref in ((wl_ref, left_ref), (wr_ref, right_ref)):
        proj = jnp.dot(weight_ref[...], feat, preferred_element_type=F32)
        for k in range(CPD):
            cut = slice(k * CL, (k + 1) * CL)
            live = (lane < fill_ref[k]).astype(F32)
            extra = jnp.concatenate(
                [high[:, cut], mid[:, cut], live, jnp.zeros((1, CL), F32)], 0
            )
            both = jnp.concatenate([proj[:, cut], extra], 0).astype(BF16)
            for peer in range(out_ref.shape[0]):
                out_ref[peer, k] = both


def unpack(block):
    extra = block[HID:]
    pos = extra[0:3] + extra[3:6]
    return block[:HID], pos, extra[6:7]


def spread4(value):
    rows, cols = value.shape
    tall = jnp.concatenate([value] * 4, 0)
    wide = jnp.concatenate([tall] * 4, 1)
    down = lax.broadcasted_iota(jnp.int32, wide.shape, 0) // rows
    across = lax.broadcasted_iota(jnp.int32, wide.shape, 1) // cols
    return jnp.where(down == across, wide, 0.0)


def tile_kernel(
    tiles_ref, count_ref, base_ref, left_ref, right_ref, wr_ref, wh_ref, wo_ref,
    first_ref, second_ref,
    tangent_ref, hidden_ref, back_ref, out_ref, pick_ref, head_ref, adds_ref,
    turned_ref, across_ref, slopes_ref, energies_ref, half1_ref, rate_ref, half2_ref, chain_ref, source_ref, target_ref, swaps_ref,
):
    count = count_ref[0]
    wide = 2 * CL
    first_ref[...] = jnp.zeros_like(first_ref)
    second_ref[...] = jnp.zeros_like(second_ref)
    w_radial = wr_ref[...].T
    radial = spread4(0.5 * w_radial)
    tangent = spread4(w_radial * (-SHARP / SCALE))
    high = tangent.astype(BF16).astype(F32)
    tangent_ref[...] = jnp.concatenate([high, tangent - high], 1).astype(BF16)
    w_hidden = wh_ref[...].astype(F32)
    w_out = wo_ref[...]
    hidden_ref[...] = spread4(0.5 * w_hidden).astype(BF16)
    back_ref[...] = spread4(w_hidden.T).astype(BF16)
    half_out = jnp.broadcast_to(jnp.concatenate([0.5 * w_out] * 4, 0), (4 * HID, wide))
    flat_out = jnp.concatenate([w_out.T] * 4, 1)
    lane8 = lax.broadcasted_iota(jnp.int32, (8, 4 * HID), 1) // HID
    sub8 = lax.broadcasted_iota(jnp.int32, (8, 4 * HID), 0)
    out_ref[...] = jnp.where(lane8 == sub8, flat_out, 0.0).astype(BF16)
    quad = lax.broadcasted_iota(jnp.int32, (HID, wide), 0) // 4
    side = lax.broadcasted_iota(jnp.int32, (HID, wide), 1) // CL
    for g in range(HID // 8):
        pick_ref[g] = (quad == 2 * g + side).astype(F32).astype(BF16)
    centers = (
        lax.broadcasted_iota(jnp.int32, (NRBF, wide), 0).astype(F32) * (RANGE / (NRBF - 1) * SCALE)
    )
    ident = (
        lax.broadcasted_iota(jnp.int32, (HID, HID), 0)
        == lax.broadcasted_iota(jnp.int32, (HID, HID), 1)
    ).astype(F32)
    lane4 = lax.broadcasted_iota(jnp.int32, (HID, CL), 1) % 4

    def prepare(slot):
        first = tiles_ref[0, slot]
        away = jnp.bitwise_xor(first // CPD, base_ref[1])
        left = left_ref[away * CPD + first % CPD].astype(F32)
        other = tiles_ref[1, slot]
        beyond = jnp.bitwise_xor(other // CPD, base_ref[3])
        right = right_ref[beyond * CPD + other % CPD].astype(F32)
        fill_left = jnp.sum(left[LIVE : LIVE + 1]).astype(jnp.int32)
        fill_right = jnp.sum(right[LIVE : LIVE + 1]).astype(jnp.int32)
        swap = fill_right < fill_left
        swaps_ref[slot] = swap.astype(jnp.int32)
        proj_a, pos_a, live_a = unpack(jnp.where(swap, right, left))
        proj_b, pos_b, live_b = unpack(jnp.where(swap, left, right))
        half_a = 0.5 * proj_a
        cols = jnp.concatenate([jnp.where(lane4 == q, half_a, 0.0) for q in range(4)], 0)
        for half in range(2):
            head_ref[slot, half] = jnp.concatenate(
                [radial, cols[:, half * HID : (half + 1) * HID], jnp.concatenate([ident] * 4, 0)], 1
            ).astype(BF16)
        adds_ref[slot] = jnp.concatenate([0.5 * proj_b] * 2, 1).astype(BF16)
        turned_ref[slot] = jnp.concatenate([pos_a, live_a, jnp.zeros((CL - 4, CL), F32)], 0).T
        across_ref[slot] = jnp.concatenate([pos_b, live_b, jnp.zeros((4, CL), F32)], 0)
        return jnp.where(slot < count, (jnp.minimum(fill_left, fill_right) + 7) // 8, 0)

    sizes = [prepare(slot) for slot in range(tiles_ref.shape[1])]
    groups = jnp.int32(0)
    for slot, size in enumerate(sizes):
        for g in range(CL // 8):
            source_ref[groups + g] = slot * 16 + g
            target_ref[groups + 2 * GROUPS + g] = slot * 16 + g
        groups = groups + size
    spare = slopes_ref.shape[0] - 1
    for k in range(2 * GROUPS):
        target_ref[k] = spare * 16
    for k in range(3 * GROUPS):
        source_ref[groups + k] = 0
        target_ref[groups + 2 * GROUPS + k] = spare * 16

    def distances(mine, across):
        delta = [mine[:, c : c + 1] - across[c : c + 1] for c in range(3)]
        dist = jnp.sqrt(delta[0] * delta[0] + delta[1] * delta[1] + delta[2] * delta[2] + SOFT)
        return delta, dist

    def place(list_ref, at):
        return list_ref[at] // 16, list_ref[at] % 16

    def enter(n):
        for e in range(GROUPS):
            slot, g = place(source_ref, n * GROUPS + e)
            mine = turned_ref[slot, pl.ds(pl.multiple_of(g * 8, 8), 8), :]
            scaled = distances(mine, across_ref[slot])[1] * SCALE
            bases = []
            rates = []
            for q in range(4):
                row = jnp.concatenate([scaled[q : q + 1], scaled[q + 4 : q + 5]], 1)
                offset = row - centers
                basis = jnp.exp2(-(offset * offset))
                bases.append(basis.astype(BF16))
                rates.append((basis * offset).astype(BF16))
            tail = jnp.concatenate(bases + [pick_ref[g % 8], adds_ref[slot]], 0)
            half1_ref[e] = jnp.dot(head_ref[slot, g // 8], tail, preferred_element_type=F32)
            rate_ref[e] = jnp.dot(
                tangent_ref[...], jnp.concatenate(rates + rates, 0), preferred_element_type=F32
            )

    def middle():
        for e in range(GROUPS):
            half1 = half1_ref[e]
            up1 = 1.0 + jnp.tanh(half1)
            silu1 = half1 * up1
            grad1 = up1 + silu1 * (2.0 - up1)
            chain_ref[e] = grad1 * rate_ref[e]
            half2_ref[e] = jnp.dot(hidden_ref[...], silu1.astype(BF16), preferred_element_type=F32)

    def leave(n):
        for e in range(GROUPS):
            slot, g = place(target_ref, n * GROUPS + e)
            half2 = half2_ref[e]
            up2 = 1.0 + jnp.tanh(half2)
            silu2 = half2 * up2
            grad2 = up2 + silu2 * (2.0 - up2)
            back1 = jnp.dot(back_ref[...], (half_out * grad2).astype(BF16), preferred_element_type=F32)
            energy = jnp.dot(out_ref[...], silu2.astype(BF16), preferred_element_type=F32)
            terms = back1 * chain_ref[e]
            lines = jnp.concatenate(
                [jnp.sum(terms[q * HID : (q + 1) * HID], 0, keepdims=True) for q in range(4)], 0
            )
            at = pl.ds(pl.multiple_of(g * 8, 8), 8)
            slopes_ref[slot, at, :] = jnp.concatenate([lines[:, :CL], lines[:, CL:]], 0)
            energies_ref[slot, at, :] = jnp.concatenate([energy[:4, :CL], energy[:4, CL:]], 0)

    def step(n, carry):
        leave(n)
        middle()
        enter(n)
        return carry

    steps = (groups + GROUPS - 1) // GROUPS
    enter(0)
    middle()
    enter(1)
    lax.fori_loop(2, steps, step, 0)
    leave(steps)
    middle()
    leave(steps + 1)

    sub = lax.broadcasted_iota(jnp.int32, (CL, CL), 0)
    lane = lax.broadcasted_iota(jnp.int32, (CL, CL), 1)
    row8 = lax.broadcasted_iota(jnp.int32, (8, CL), 0) // 4

    def finish(slot, carry):
        first = tiles_ref[0, slot]
        other = tiles_ref[1, slot]
        same = base_ref[0] + first == (other // CPD * base_ref[2] + base_ref[1]) * CPD + other % CPD
        mine = turned_ref[slot]
        across = across_ref[slot]
        delta, dist = distances(mine, across)
        mask = mine[:, 3:4] * across[3:4] * (slot < count).astype(F32)
        keep = jnp.logical_and(mask > 0.0, jnp.logical_or(jnp.logical_not(same), sub != lane))
        weight = jnp.where(keep, slopes_ref[slot] / dist, 0.0)
        pulls = [weight * d for d in delta]
        kept = jnp.where(keep, energies_ref[slot], 0.0)
        down = jnp.concatenate(
            [-jnp.sum(p.T, 0, keepdims=True) for p in pulls] + [jnp.sum(kept.T, 0, keepdims=True)], 0
        )
        along = jnp.concatenate([jnp.sum(p, 0, keepdims=True) for p in pulls + [kept]], 0)
        swap = swaps_ref[slot] == 1
        firsts = jnp.where(swap, along, down)
        seconds = jnp.where(swap, down, along)
        away = jnp.bitwise_xor(first // CPD, base_ref[1])
        first_ref[away % 4 * 4 + away // 4] += jnp.where(row8 == first % CPD, jnp.concatenate([firsts] * 2, 0), 0.0)
        second_ref[other // CPD] += jnp.where(
            row8 == other % CPD, jnp.concatenate([seconds] * 2, 0), 0.0
        )
        return carry

    for slot in range(tiles_ref.shape[1]):
        finish(slot, 0)


def tile_call(tiles, tile_count, base, left, right, w_radial, w_hidden, w_out):
    smem = pl.BlockSpec(memory_space=pltpu.SMEM)
    vmem = pl.BlockSpec(memory_space=pltpu.VMEM)
    slots = tiles.shape[0]
    groups = GROUPS
    listed = (slots + 1) * (CL // 8) + 5 * GROUPS
    hid4 = 4 * HID
    wide = 2 * CL
    return pl.pallas_call(
        tile_kernel,
        name="tiles",
        out_shape=(
            jax.ShapeDtypeStruct((left.shape[0] // CPD, 8, CL), F32),
            jax.ShapeDtypeStruct((right.shape[0] // CPD, 8, CL), F32),
        ),
        in_specs=[smem] * 3 + [vmem] * 5,
        out_specs=(vmem, vmem),
        scratch_shapes=[
            pltpu.VMEM((hid4, 8 * NRBF), BF16),
            pltpu.VMEM((hid4, hid4), BF16),
            pltpu.VMEM((hid4, hid4), BF16),
            pltpu.VMEM((8, hid4), BF16),
            pltpu.VMEM((HID // 8, HID, wide), BF16),
            pltpu.VMEM((slots, 2, hid4, hid4), BF16),
            pltpu.VMEM((slots, HID, wide), BF16),
            pltpu.VMEM((slots, CL, CL), F32),
            pltpu.VMEM((slots, 8, CL), F32),
            pltpu.VMEM((slots + 1, CL, CL), F32),
            pltpu.VMEM((slots + 1, CL, CL), F32),
            pltpu.VMEM((groups, hid4, wide), F32),
            pltpu.VMEM((groups, hid4, wide), F32),
            pltpu.VMEM((groups, hid4, wide), F32),
            pltpu.VMEM((groups, hid4, wide), F32),
            pltpu.SMEM((listed,), jnp.int32),
            pltpu.SMEM((listed,), jnp.int32),
            pltpu.SMEM((slots,), jnp.int32),
        ],
        compiler_params=pltpu.CompilerParams(vmem_limit_bytes=48 * 1024 * 1024),
    )(
        tiles.T, tile_count, base, left, right, w_radial.T, w_hidden, w_out.astype(F32)[:, None],
    )


def across(count, step):
    return [(i, i ^ step) for i in range(count)]


def add_kernel(own_ref, one_ref, two_ref, three_ref, second_ref, force_ref, energy_ref):
    total = own_ref[...] + one_ref[...] + two_ref[...] + three_ref[...]
    other = second_ref[0]
    for peer in range(1, second_ref.shape[0]):
        other = other + second_ref[peer]
    force = total + other
    for k in range(CPD):
        cut = slice(k * CL, (k + 1) * CL)
        force_ref[:, cut] = force[4 * k : 4 * k + 3]
        energy_ref[:, cut] = total[4 * k + 3 : 4 * k + 4]


def body(positions, features, fill, tiles, tile_count, w_radial, w_left, w_right, w_hidden, w_out):
    rows = lax.axis_size("row")
    cols = lax.axis_size("col")
    smem = pl.BlockSpec(memory_space=pltpu.SMEM)
    vmem = pl.BlockSpec(memory_space=pltpu.VMEM)
    with jax.named_scope("pack"):
        left, right = pl.pallas_call(
            pack_kernel,
            out_shape=(
                jax.ShapeDtypeStruct((1, CPD, PAY, CL), BF16),
                jax.ShapeDtypeStruct((1, CPD, PAY, CL), BF16),
            ),
            in_specs=[smem] + [vmem] * 4,
            out_specs=(vmem, vmem),
        )(fill, positions, features, w_left.T, w_right.T)
    with jax.named_scope("spread"):
        left, right = [
            jnp.concatenate([own] + [lax.ppermute(own, axis, across(16, k)) for k in range(1, 4)], 0)
            for own, axis in ((left, "col"), (right, "row"))
        ]
        left, right = [
            jnp.concatenate([own] + [lax.ppermute(own, axis, across(16, 4 * k)) for k in range(1, 4)], 0)
            .reshape(16 * CPD, PAY, CL)
            for own, axis in ((left, "col"), (right, "row"))
        ]
    base = jnp.stack(
        [lax.axis_index("row") * cols * CPD, lax.axis_index("col"), jnp.int32(cols), lax.axis_index("row")]
    )
    with jax.named_scope("tiles"):
        firsts, seconds = tile_call(
            tiles, tile_count, base, left, right, w_radial, w_hidden, w_out
        )
    with jax.named_scope("collect"):
        seconds = lax.all_to_all(seconds, "row", 0, 0)
        firsts = firsts.reshape(4, 4, 8, CL)
        near = firsts[0]
        for k in range(1, 4):
            near = near + lax.ppermute(firsts[k], "col", across(cols, k))
        firsts = [near[0]] + [lax.ppermute(near[k], "col", across(cols, 4 * k)) for k in range(1, 4)]
    with jax.named_scope("add"):
        force, energy = pl.pallas_call(
            add_kernel,
            out_shape=(
                jax.ShapeDtypeStruct((3, CPD * CL), F32),
                jax.ShapeDtypeStruct((1, CPD * CL), F32),
            ),
        )(*firsts, seconds)
    return force, energy.reshape(CPD * CL)


def solution(mesh):
    return jax.shard_map(
        body,
        mesh=mesh,
        in_specs=(
            P(None, ("row", "col")),
            P(None, ("row", "col")),
            P(("row", "col")),
            P(("row", "col"), None),
            P(("row", "col")),
            P(),
            P(),
            P(),
            P(),
            P(),
        ),
        out_specs=(P(None, ("row", "col")), P(("row", "col"))),
        check_vma=False,
    )
```
